256 devices in a mesh: expert: 64 (over x, z, core), pipe: 4 (over y).
Axes of the slice: x: 4, y: 4, z: 8, core: 2. Of those that a mesh axis runs over, the one named last changes fastest.
Arguments:
- section_input: bfloat16 [4, 8192, 7168], P('pipe', 'expert'), may hold values from -6 to 6
- cotangent: bfloat16 [4, 8192, 7168], P('pipe', 'expert'), may hold values from -6 to 6
- routes: int32 [4, 8192, 8], P('pipe', 'expert'), may hold values from 0 to 255, as said below
- gate_codes: int32 [4, 8192, 8], P('pipe', 'expert'), may hold values from 1 to 256
- w_gate: bfloat16 [4, 7168, 8192], P('pipe', None, 'expert'), may hold values from -0.0625 to 0.0625
- w_up: bfloat16 [4, 7168, 8192], P('pipe', None, 'expert'), may hold values from -0.0625 to 0.0625
- w_down: bfloat16 [4, 8192, 7168], P('pipe', 'expert'), may hold values from -0.125 to 0.125
Outputs:
- next_section_input: bfloat16 [4, 8192, 7168], P('pipe', 'expert')
- prev_section_grad: bfloat16 [4, 8192, 7168], P('pipe', 'expert')
The draws below stay inside these ranges and needn't reach their ends.
Inputs may be any that keep to these rules, and one draw needn't show every extreme that they name: `routes`: each token names 8 different experts. Of the 128 tokens of one block, at most 4 name any one expert below 4; in every section some expert below 4 is named by exactly 4 tokens of every block.
All inputs are finite; a program needn't handle non-finite values.
Results may differ from the reference program's by a relative error of at most 0.011.
Values may be sent and summed in bfloat16 or wider, within the bound.
A program may use at most 128 MiB of HBM per device.

```python
import jax
import jax.numpy as jnp
from jax import lax

D = 7168
FF = 2048
EXPERTS = 256
TOP = 8
TOK_DEV = 128
SECTIONS = 4
TOKENS = 8192
GROUP = 16
FLIGHT = 4
H_DEV = 128
CAP = 4


def draw_routes(key, part):
    key = jax.random.fold_in(key, 7)
    subkeys = jax.random.split(key, 5)
    per_section = TOKENS // TOK_DEV
    blocks = SECTIONS * per_section
    hottest = jax.random.randint(subkeys[0], (SECTIONS,), 0, FLIGHT)
    counts = jax.random.randint(subkeys[1], (blocks, FLIGHT), 0, CAP)
    section_of = jnp.arange(blocks) // per_section
    counts = jnp.where(jnp.arange(FLIGHT)[None, :] == hottest[section_of][:, None], CAP, counts)
    scores = jax.random.randint(subkeys[2], (blocks, FLIGHT, TOK_DEV), 0, 2 ** 20) * TOK_DEV + jnp.arange(TOK_DEV)
    ranking = jnp.argsort(jnp.argsort(scores, axis=-1), axis=-1)
    member = (ranking < counts[:, :, None]).astype(jnp.int32)
    member = jnp.transpose(member, (0, 2, 1))
    running = jnp.cumsum(member, axis=-1)
    inside = running[:, :, -1:]
    slot_ids = jnp.arange(TOP)
    chosen = jnp.sum(jnp.arange(FLIGHT)[None, None, None, :] * member[:, :, None, :] * (running[:, :, None, :] - 1 == slot_ids[None, None, :, None]), axis=-1)
    offset = jax.random.randint(subkeys[3], (blocks, TOK_DEV, 1), 0, EXPERTS - FLIGHT)
    others = FLIGHT + (offset + slot_ids) % (EXPERTS - FLIGHT)
    listed = jnp.where(slot_ids[None, None, :] < inside, chosen, others)
    rotation = jax.random.randint(subkeys[4], (blocks, TOK_DEV, 1), 0, TOP)
    position = (slot_ids - rotation) % TOP
    rolled_ids = jnp.take_along_axis(listed, position, axis=-1)
    return rolled_ids.reshape(SECTIONS, TOKENS, TOP).astype(jnp.int32)


def with_ends(array, key, low, top_value):
    longest = array.shape.index(max(array.shape))
    spots = []
    for shift in (0, 1):
        where = [jax.random.randint(jax.random.fold_in(key, axis), (), 0, length) for axis, length in enumerate(array.shape)]
        where[longest] = (where[longest] + shift) % array.shape[longest]
        spots.append(tuple(where))
    return array.at[spots[0]].set(low).at[spots[1]].set(top_value)


def block_scale(key, shape, cuts, low, top_value):
    gain = 1.0
    for dim, parts in cuts:
        steps = jax.random.uniform(jax.random.fold_in(jax.random.fold_in(key, 6), dim), (parts,), jnp.float32, low / len(cuts), top_value / len(cuts))
        gain = gain * jnp.repeat(jnp.exp(steps), shape[dim] // parts).reshape((-1,) + (1,) * (len(shape) - 1 - dim))
    return gain


def gaussian(stream_key, shape, scale, limit, cuts=(), kind=jnp.bfloat16):
    entries = scale * jax.random.normal(stream_key, shape, jnp.float32)
    if cuts:
        entries = entries * block_scale(stream_key, shape, cuts, -0.22, 0.18)
    return jnp.clip(entries, -limit, limit).astype(kind)


def setup_inputs(seed: int = 0) -> dict:
    key_of = jax.random.split(jax.random.key(seed), 8)
    return {
        "section_input": gaussian(key_of[0], (SECTIONS, TOKENS, D), 1.0, 6.0, ((0, 4), (1, 64))),
        "cotangent": gaussian(key_of[1], (SECTIONS, TOKENS, D), 1.0, 6.0, ((0, 4), (1, 64))),
        "routes": draw_routes(jax.random.fold_in(key_of[7], 71), 0),
        "gate_codes": with_ends(jax.random.randint(key_of[3], (SECTIONS, TOKENS, TOP), 1, 257), jax.random.fold_in(key_of[3], 1), 1, 256).astype(jnp.int32),
        "w_gate": gaussian(key_of[4], (SECTIONS, D, FLIGHT * FF), D ** -0.5, 0.0625, ((0, 4), (2, 64))),
        "w_up": gaussian(key_of[5], (SECTIONS, D, FLIGHT * FF), D ** -0.5, 0.0625, ((0, 4), (2, 64))),
        "w_down": gaussian(key_of[6], (SECTIONS, FLIGHT * FF, D), FF ** -0.5, 0.125, ((0, 4), (1, 64))),
    }


def reference(section_input, cotangent, routes, gate_codes, w_gate, w_up, w_down):
    highest = lax.Precision.HIGHEST
    blocks = TOKENS // TOK_DEV
    row_count = blocks * CAP
    codes_float = gate_codes.astype(jnp.float32)
    route_weight = 2.5 * codes_float / jnp.sum(codes_float, axis=-1, keepdims=True)
    slot_ids = jnp.arange(CAP, dtype=jnp.int32)
    expert_ids = jnp.arange(FLIGHT, dtype=jnp.int32)
    layer_list = []
    grad_list = []
    for section_index in range(SECTIONS):
        tokens_in = section_input[section_index].reshape(blocks, TOK_DEV, D).astype(jnp.float32)
        grads_in = cotangent[section_index].reshape(blocks, TOK_DEV, D).astype(jnp.float32)
        named = routes[section_index].reshape(blocks, TOK_DEV, TOP, 1) == expert_ids
        matched = jnp.sum(named, axis=2).astype(jnp.int32)
        token_weight = jnp.sum(jnp.where(named, route_weight[section_index].reshape(blocks, TOK_DEV, TOP, 1), 0.0), axis=2)
        position = jnp.cumsum(matched, axis=1) - 1
        selector = ((matched[:, None, :, :] == 1) & (position[:, None, :, :] == slot_ids[None, :, None, None])).astype(jnp.float32)
        rows = jnp.einsum("bctf,btd->fbcd", selector, tokens_in, precision=highest).astype(jnp.bfloat16)
        rows = rows.reshape(FLIGHT, row_count, D)
        slot_weight = jnp.einsum("bctf,btf->fbc", selector, token_weight, precision=highest)
        grad_slots = jnp.einsum("bctf,btd->fbcd", selector, grads_in, precision=highest)
        out_grad = (slot_weight[..., None] * grad_slots).astype(jnp.bfloat16).reshape(FLIGHT, row_count, D)
        expert_outs = []
        expert_grads = []
        for expert in range(FLIGHT):
            gate_block = w_gate[section_index][:, expert * FF:(expert + 1) * FF].astype(jnp.float32)
            up_block = w_up[section_index][:, expert * FF:(expert + 1) * FF].astype(jnp.float32)
            down_block = w_down[section_index][expert * FF:(expert + 1) * FF, :].astype(jnp.float32)
            row_data = rows[expert].astype(jnp.float32)
            gate = jnp.dot(row_data, gate_block, precision=highest)
            upper = jnp.dot(row_data, up_block, precision=highest)
            hidden = (jax.nn.silu(gate) * upper).astype(jnp.bfloat16)
            slice_out = jnp.einsum("rgh,ghd->grd", hidden.astype(jnp.float32).reshape(row_count, GROUP, H_DEV),
                                   down_block.reshape(GROUP, H_DEV, D), precision=highest).astype(jnp.bfloat16)
            slice_out = lax.optimization_barrier(slice_out)
            expert_outs.append(jnp.sum(slice_out.astype(jnp.float32), axis=0))
            d_hidden = jnp.dot(out_grad[expert].astype(jnp.float32), down_block.T, precision=highest)
            sigma = jax.nn.sigmoid(gate)
            d_gate = (d_hidden * upper * sigma * (1.0 + gate * (1.0 - sigma))).astype(jnp.bfloat16)
            d_up = (d_hidden * jax.nn.silu(gate)).astype(jnp.bfloat16)
            slice_grad = jnp.einsum("rgh,dgh->grd", d_gate.astype(jnp.float32).reshape(row_count, GROUP, H_DEV),
                                    gate_block.reshape(D, GROUP, H_DEV), precision=highest)
            slice_grad = slice_grad + jnp.einsum("rgh,dgh->grd", d_up.astype(jnp.float32).reshape(row_count, GROUP, H_DEV),
                                                 up_block.reshape(D, GROUP, H_DEV), precision=highest)
            slice_grad = lax.optimization_barrier(slice_grad.astype(jnp.bfloat16))
            expert_grads.append(jnp.sum(slice_grad.astype(jnp.float32), axis=0))
        summed_out = jnp.stack(expert_outs).reshape(FLIGHT, blocks, CAP, D)
        summed_grad = jnp.stack(expert_grads).reshape(FLIGHT, blocks, CAP, D)
        weighted = summed_out * slot_weight[..., None]
        layer_out = jnp.einsum("bctf,fbcd->btd", selector, weighted, precision=highest)
        input_grad = jnp.einsum("bctf,fbcd->btd", selector, summed_grad, precision=highest)
        layer_list.append(layer_out.reshape(TOKENS, D).astype(jnp.bfloat16))
        grad_list.append(input_grad.reshape(TOKENS, D).astype(jnp.bfloat16))
    layer_all = jnp.stack(layer_list)
    grad_all = jnp.stack(grad_list)
    return jnp.roll(layer_all, 1, axis=0), jnp.roll(grad_all, -1, axis=0)
```

```python
import jax
import jax.numpy as jnp
from jax import lax
from jax.sharding import PartitionSpec as P

FF = 2048
CAP = 4
FLIGHT = 4


def contract_rows(left, right):
    return lax.dot_general(
        left, right, (((1,), (1,)), ((), ())), preferred_element_type=jnp.float32
    )


def on_device(section_input, cotangent, routes, gate_codes, w_gate, w_up, w_down):
    highest = lax.Precision.HIGHEST
    tokens_in = section_input[0]
    grads_in = cotangent[0]
    route_ids = routes[0]
    codes_float = gate_codes[0].astype(jnp.float32)
    gate_cols = w_gate[0]
    up_cols = w_up[0]
    down_rows = w_down[0]
    devices = lax.axis_size("expert")
    group = devices // FLIGHT
    width = tokens_in.shape[1]
    across = [[f * group + i for f in range(FLIGHT)] for i in range(group)]
    along = [[f * group + i for i in range(group)] for f in range(FLIGHT)]
    route_weight = 2.5 * codes_float / jnp.sum(codes_float, axis=-1, keepdims=True)
    named = route_ids[:, :, None] == jnp.arange(FLIGHT, dtype=jnp.int32)
    matched = jnp.sum(named, axis=1)
    token_weight = jnp.sum(jnp.where(named, route_weight[:, :, None], 0.0), axis=1)
    position = jnp.cumsum(matched, axis=0) - 1
    selector = (matched.T[:, None, :] == 1) & (
        position.T[:, None, :] == jnp.arange(CAP, dtype=jnp.int32)[None, :, None]
    )
    slots = FLIGHT * CAP
    picks = selector.astype(jnp.bfloat16).reshape(slots, -1)
    picks_wide = selector.astype(jnp.float32)
    send_rows = jnp.dot(picks, tokens_in, preferred_element_type=jnp.float32).astype(jnp.bfloat16)
    slot_weight = jnp.einsum("fct,tf->fc", picks_wide, token_weight, precision=highest).reshape(slots)
    picks_wide = picks_wide.reshape(slots, -1)
    grad_slots = jnp.dot(picks, grads_in, preferred_element_type=jnp.float32)
    send_grads = (slot_weight[:, None] * grad_slots).astype(jnp.bfloat16)
    same = jnp.dot(picks_wide, picks_wide.T, precision=highest)
    earlier = jnp.tril(same, -1)
    first = (jnp.sum(earlier, axis=1) == 0).astype(jnp.float32)
    merge = first[:, None] * same
    place = (picks_wide * first[:, None]).astype(jnp.bfloat16)

    def gather(block):
        here = lax.all_to_all(
            block.reshape(FLIGHT, CAP, width), "expert", split_axis=0, concat_axis=0,
            axis_index_groups=across, tiled=True,
        )
        return lax.all_gather(
            here.reshape(slots, width), "expert", axis_index_groups=along, tiled=True
        )

    def reduce(block):
        here = lax.psum_scatter(
            block, "expert", scatter_dimension=0, axis_index_groups=along, tiled=True
        )
        return lax.all_to_all(
            here.reshape(FLIGHT, CAP, width), "expert", split_axis=0, concat_axis=0,
            axis_index_groups=across, tiled=True,
        ).reshape(slots, width)

    rows = gather(send_rows)
    gate = jnp.dot(rows, gate_cols, preferred_element_type=jnp.float32)
    upper = jnp.dot(rows, up_cols, preferred_element_type=jnp.float32)
    hidden = (jax.nn.silu(gate) * upper).astype(jnp.bfloat16)
    partial_value = jnp.dot(hidden, down_rows, preferred_element_type=jnp.float32).astype(
        jnp.bfloat16
    )
    grad_rows = gather(send_grads)
    out_sum = reduce(partial_value)
    d_hidden = contract_rows(grad_rows, down_rows)
    sigma = jax.nn.sigmoid(gate)
    d_gate = (d_hidden * upper * sigma * (1.0 + gate * (1.0 - sigma))).astype(jnp.bfloat16)
    d_up = (d_hidden * jax.nn.silu(gate)).astype(jnp.bfloat16)
    grad_part = (contract_rows(d_gate, gate_cols) + contract_rows(d_up, up_cols)).astype(
        jnp.bfloat16
    )
    grad_sum = reduce(grad_part)
    layer_out = jnp.dot(
        merge * slot_weight[None, :], out_sum.astype(jnp.float32), precision=highest
    ).astype(jnp.bfloat16)
    input_grad = jnp.dot(merge, grad_sum.astype(jnp.float32), precision=highest).astype(
        jnp.bfloat16
    )
    pipes = lax.axis_size("pipe")
    ahead = [(i, (i + 1) % pipes) for i in range(pipes)]
    back = [(i, (i - 1) % pipes) for i in range(pipes)]

    def spread(block, route):
        there = lax.ppermute(block, "pipe", route)
        where = lax.ppermute(place, "pipe", route)
        return lax.dot_general(
            where, there, (((0,), (0,)), ((), ())), preferred_element_type=jnp.float32
        ).astype(jnp.bfloat16)[None]

    return (spread(layer_out, ahead), spread(input_grad, back))


def solution(mesh):
    placed = (
        P("pipe", "expert", None),
        P("pipe", "expert", None),
        P("pipe", "expert", None),
        P("pipe", "expert", None),
        P("pipe", None, "expert"),
        P("pipe", None, "expert"),
        P("pipe", "expert", None),
    )
    return jax.shard_map(
        on_device,
        mesh=mesh,
        in_specs=placed,
        out_specs=(P("pipe", "expert", None), P("pipe", "expert", None)),
        check_vma=False,
    )
```

```python
import jax
import jax.numpy as jnp
from jax import lax
from jax.experimental import pallas as pl
from jax.experimental.pallas import tpu as pltpu
from jax.sharding import PartitionSpec as P

CAP = 4
FLIGHT = 4
SLOTS = FLIGHT * CAP
CORES = 2
QUARTERS = 4
RING = 8
HOPS = 7
TILE = 512
MESH = pl.DeviceIdType.MESH
F32 = jnp.float32
BF16 = jnp.bfloat16

RIGHT, LEFT = 0, 1
FROM = {RIGHT: (0, 1, 3, 5, 7), LEFT: (0, 2, 4, 6, 7)}
GATHER = {
    RIGHT: ((0, 0), (0, 1), (1, 0), (1, 1), (2, 0), (2, 1), (3, 0)),
    LEFT: ((0, 1), (0, 0), (1, 1), (1, 0), (2, 1), (2, 0), (3, 1)),
}
REDUCE = {
    LEFT: ((4, 0), (3, 1), (3, 0), (2, 1), (2, 0), (1, 1), (1, 0)),
    RIGHT: ((4, 1), (3, 0), (3, 1), (2, 0), (2, 1), (1, 0), (1, 1)),
}


def nt(left, right):
    return lax.dot_general(left, right, (((1,), (1,)), ((), ())), preferred_element_type=F32)


def tn(left, right):
    return lax.dot_general(left, right, (((0,), (0,)), ((), ())), preferred_element_type=F32)


def regroup(q):
    row = lax.broadcasted_iota(jnp.int32, (SLOTS, SLOTS * QUARTERS), 0)
    col = lax.broadcasted_iota(jnp.int32, (SLOTS, SLOTS * QUARTERS), 1)
    there = (row & ~3) * QUARTERS + (row & 3) + q * CAP
    return (col == there).astype(F32).astype(BF16)


def exchange(
    x_ref, g_ref, wy_ref, sel_ref, wg_ref, wu_ref, wd_ref,
    out_y, out_g, out_wy, out_sel,
    stage_x, stage_g, rows, grads, gu, wd, acc, a_gate, a_up, hid, dh, dgu,
    part_y, part_g, recv_y, recv_g, fin_y, fin_g,
    local_sems, w_send, w_recv, x_send, x_recv, s_send, s_recv,
    ring_send, ring_recv, fin_send, fin_recv,
):
    me = lax.axis_index("expert")
    y = lax.axis_index("pipe")
    pipes = lax.axis_size("pipe")
    core = lax.rem(me, CORES)
    z = lax.rem(lax.div(me, CORES), RING)
    x = lax.div(me, CORES * RING)
    width = wd.shape[1]
    half = width // 2
    quarter = width // QUARTERS
    units = wg_ref.shape[1]

    def at(xx, zz, cc, yy):
        return ((xx * RING + zz) * CORES + cc, yy)

    ahead = lax.rem(y + 1, pipes)
    behind = lax.rem(y + pipes - 1, pipes)
    sibling = at(x, z, 1 - core, y)
    next_on = {
        RIGHT: at(x, lax.rem(z + 1, RING), core, y),
        LEFT: at(x, lax.rem(z + RING - 1, RING), core, y),
    }
    across = [at(lax.rem(x + k, FLIGHT), z, core, y) for k in range(FLIGHT)]
    up = [at(lax.rem(x + k, FLIGHT), z, core, ahead) for k in range(FLIGHT)]
    down = [at(lax.rem(x + k, FLIGHT), z, core, behind) for k in range(FLIGHT)]

    own = [
        pltpu.make_async_copy(wg_ref, gu.at[:, pl.ds(0, units)], local_sems.at[0]),
        pltpu.make_async_copy(wu_ref, gu.at[:, pl.ds(2 * units, units)], local_sems.at[1]),
        pltpu.make_async_copy(wd_ref, wd.at[pl.ds(0, units)], local_sems.at[2]),
    ]
    for copy in own:
        copy.start()

    barrier = pltpu.get_barrier_semaphore()
    peers = [sibling, next_on[RIGHT], next_on[LEFT]] + across[1:] + up + down
    for peer in peers:
        pl.semaphore_signal(barrier, inc=1, device_id=peer, device_id_type=MESH)
    pl.semaphore_wait(barrier, len(peers))

    def remote(src, dst, send, recv, device):
        return pltpu.make_async_remote_copy(
            src_ref=src, dst_ref=dst, send_sem=send, recv_sem=recv,
            device_id=device, device_id_type=MESH,
        )

    x_copies = []
    for i, (src, stage) in enumerate(((x_ref, stage_x), (g_ref, stage_g))):
        x_copies.append([
            remote(src.at[lax.rem(x + k, FLIGHT)], stage.at[x], x_send.at[i, k], x_recv.at[i, k], across[k])
            for k in range(1, FLIGHT)
        ])
    for copy in x_copies[0] + x_copies[1]:
        copy.start()
    stage_x[x] = x_ref[x]
    stage_g[x] = g_ref[x]
    small = [
        remote(wy_ref, out_wy, s_send.at[0], s_recv.at[0], up[0]),
        remote(sel_ref, out_sel, s_send.at[1], s_recv.at[1], down[0]),
    ]
    other = [
        remote(wg_ref, gu.at[:, pl.ds(units, units)], w_send.at[0], w_recv.at[0], sibling),
        remote(wu_ref, gu.at[:, pl.ds(3 * units, units)], w_send.at[1], w_recv.at[1], sibling),
        remote(wd_ref, wd.at[pl.ds(units, units)], w_send.at[2], w_recv.at[2], sibling),
    ]
    for copy in other + small:
        copy.start()

    def natural(stage, dst):
        def body(i, carry):
            cols = pl.ds(pl.multiple_of(i * 256, 256), 256)
            block = stage[:, :, cols].reshape(SLOTS * QUARTERS, 256)
            for q in range(QUARTERS):
                got = jnp.dot(regroup(q), block, preferred_element_type=F32)
                dst[pl.ds(0, SLOTS), pl.ds(pl.multiple_of(q * quarter + i * 256, 256), 256)] = got.astype(BF16)
            return carry
        lax.fori_loop(0, quarter // 256, body, 0)

    def block_of(buf, place, h):
        return buf.at[pl.ds(SLOTS * place, SLOTS), pl.ds(half * h, half)]

    def gather_copy(kind, buf, way, k):
        distance, h = GATHER[way][k]
        return remote(
            block_of(buf, FROM[way][distance], h), block_of(buf, FROM[way][distance + 1], h),
            ring_send.at[kind, way, k], ring_recv.at[kind, way, k], next_on[way],
        )

    def gather_step(kind, buf, k):
        for way in (RIGHT, LEFT):
            if k >= 2:
                gather_copy(kind, buf, way, k - 2).wait_recv()
            gather_copy(kind, buf, way, k).start()

    def gather_end(kind, buf):
        for k in (HOPS - 2, HOPS - 1):
            for way in (RIGHT, LEFT):
                gather_copy(kind, buf, way, k).wait_recv()

    def reduce_copy(kind, part, recv, way, k):
        distance, h = REDUCE[way][k]
        return remote(
            block_of(part, FROM[1 - way][distance], h), recv.at[way, k],
            ring_send.at[kind, way, k], ring_recv.at[kind, way, k], next_on[way],
        )

    def reduce_step(kind, part, recv, k):
        for way in (RIGHT, LEFT):
            if k >= 2:
                reduce_copy(kind, part, recv, way, k - 2).wait_recv()
                distance, h = REDUCE[way][k]
                place = FROM[1 - way][distance]
                rs, cs = pl.ds(SLOTS * place, SLOTS), pl.ds(half * h, half)
                part[rs, cs] = (part[rs, cs].astype(F32) + recv[way, k - 2].astype(F32)).astype(BF16)
            reduce_copy(kind, part, recv, way, k).start()

    def finish(kind, part, recv, fin, out, targets, i):
        for k in (HOPS - 2, HOPS - 1):
            for way in (RIGHT, LEFT):
                reduce_copy(kind, part, recv, way, k).wait_recv()
        for h in range(2):
            from_left = HOPS - 2 if REDUCE[LEFT][HOPS - 2][1] == h else HOPS - 1
            from_right = HOPS - 2 if REDUCE[RIGHT][HOPS - 2][1] == h else HOPS - 1
            rs, cs = pl.ds(0, SLOTS), pl.ds(half * h, half)
            total = part[rs, cs].astype(F32) + recv[LEFT, from_left].astype(F32)
            part[rs, cs] = (total + recv[RIGHT, from_right].astype(F32)).astype(BF16)

        def body(j, carry):
            cols = pl.ds(pl.multiple_of(j * 256, 256), 256)
            got = jnp.zeros((SLOTS * QUARTERS, 256), F32)
            for q in range(QUARTERS):
                block = part[pl.ds(0, SLOTS), pl.ds(pl.multiple_of(q * quarter + j * 256, 256), 256)]
                got += tn(regroup(q), block)
            fin[:, :, cols] = got.astype(BF16).reshape(FLIGHT, SLOTS, 256)
            return carry
        lax.fori_loop(0, quarter // 256, body, 0)
        copies = [
            remote(fin.at[lax.rem(x + k, FLIGHT)], out.at[x], fin_send.at[i, k], fin_recv.at[i, k], targets[k])
            for k in range(FLIGHT)
        ]
        for copy in copies:
            copy.start()
        return copies

    def gate_up(first, last):
        def body(i, carry):
            ks = pl.ds(pl.multiple_of(i * TILE, TILE), TILE)
            acc[...] += jnp.dot(rows[:, ks], gu[ks, :], preferred_element_type=F32)
            return carry
        lax.fori_loop(first, last, body, 0)

    def activate():
        gate, upper = acc[:, : 2 * units], acc[:, 2 * units :]
        sigma = jax.nn.sigmoid(gate)
        silu = gate * sigma
        hid[...] = (silu * upper).astype(BF16)
        a_gate[...] = upper * sigma * (1.0 + gate * (1.0 - sigma))
        a_up[...] = silu

    def outputs(first, last):
        def body(i, carry):
            cols = pl.ds(pl.multiple_of(i * TILE, TILE), TILE)
            part_y[:, cols] = jnp.dot(hid[...], wd[:, cols], preferred_element_type=F32).astype(BF16)
            return carry
        lax.fori_loop(first, last, body, 0)

    def d_hidden(first, last):
        def body(i, carry):
            ks = pl.ds(pl.multiple_of(i * TILE, TILE), TILE)
            dh[...] += nt(grads[:, ks], wd[:, ks])
            return carry
        lax.fori_loop(first, last, body, 0)

    def d_inputs(first, last):
        def body(i, carry):
            cols = pl.ds(pl.multiple_of(i * TILE, TILE), TILE)
            part_g[:, cols] = nt(dgu[...], gu[cols, :]).astype(BF16)
            return carry
        lax.fori_loop(first, last, body, 0)

    tiles = width // TILE

    for copy in x_copies[0]:
        copy.wait_recv()
    natural(stage_x, rows)
    gather_step(0, rows, 0)
    gather_step(0, rows, 1)
    for copy in x_copies[1]:
        copy.wait_recv()
    natural(stage_g, grads)
    acc[...] = jnp.zeros_like(acc)
    dh[...] = jnp.zeros_like(dh)
    for k in range(2, HOPS):
        gather_step(0, rows, k)

    gather_step(1, grads, 0)
    gather_step(1, grads, 1)
    gather_end(0, rows)
    for copy in own:
        copy.wait()
    for copy in other:
        copy.wait_recv()
    gate_up(0, tiles // 2)
    gather_step(1, grads, 2)
    gate_up(tiles // 2, tiles)
    gather_step(1, grads, 3)
    activate()
    outputs(0, tiles // 2)
    gather_step(1, grads, 4)
    outputs(tiles // 2, tiles)
    gather_step(1, grads, 5)
    gather_step(1, grads, 6)

    reduce_step(2, part_y, recv_y, 0)
    reduce_step(2, part_y, recv_y, 1)
    gather_end(1, grads)
    d_hidden(0, tiles)
    reduce_step(2, part_y, recv_y, 2)
    dgu[:, : 2 * units] = (dh[...] * a_gate[...]).astype(BF16)
    dgu[:, 2 * units :] = (dh[...] * a_up[...]).astype(BF16)
    d_inputs(0, tiles // 2)
    reduce_step(2, part_y, recv_y, 3)
    d_inputs(tiles // 2, tiles)
    for k in range(4, HOPS):
        reduce_step(2, part_y, recv_y, k)

    reduce_step(3, part_g, recv_g, 0)
    reduce_step(3, part_g, recv_g, 1)
    done = finish(2, part_y, recv_y, fin_y, out_y, up, 0)
    for k in range(2, HOPS):
        reduce_step(3, part_g, recv_g, k)
    done += finish(3, part_g, recv_g, fin_g, out_g, down, 1)

    for copy in x_copies[0] + x_copies[1] + other:
        copy.wait_send()
    for copy in small + done:
        copy.wait()
    for k in range(HOPS):
        for way in (RIGHT, LEFT):
            gather_copy(0, rows, way, k).wait_send()
            gather_copy(1, grads, way, k).wait_send()
            reduce_copy(2, part_y, recv_y, way, k).wait_send()
            reduce_copy(3, part_g, recv_g, way, k).wait_send()


def place_kernel(y_ref, g_ref, wy_ref, sel_ref, out_ref, grad_ref):
    q = pl.program_id(0)
    row = lax.broadcasted_iota(jnp.int32, wy_ref.shape, 0)
    mine = ((row // CAP) & (QUARTERS - 1)) == q
    weight = jnp.where(mine, wy_ref[...], 0.0)
    high = weight.astype(BF16)
    rest = weight - high.astype(F32)
    mid = rest.astype(BF16)
    low = (rest - mid.astype(F32)).astype(BF16)
    block = y_ref[...].reshape(SLOTS * QUARTERS, -1)
    total = tn(jnp.concatenate([high, mid, low], axis=0), jnp.concatenate([block] * 3, axis=0))
    out_ref[...] = total.astype(BF16)
    pick = jnp.where(mine, sel_ref[...], 0.0).astype(BF16)
    grad_ref[...] = tn(pick, g_ref[...].reshape(SLOTS * QUARTERS, -1)).astype(BF16)


def on_device(section_input, cotangent, routes, gate_codes, w_gate, w_up, w_down):
    highest = lax.Precision.HIGHEST
    tokens_in = section_input[0]
    grads_in = cotangent[0]
    route_ids = routes[0]
    codes_float = gate_codes[0].astype(F32)
    tokens, width = tokens_in.shape
    quarter = width // QUARTERS
    half = width // 2
    units = w_gate.shape[2]
    route_weight = 2.5 * codes_float / jnp.sum(codes_float, axis=-1, keepdims=True)
    named = route_ids[:, :, None] == jnp.arange(FLIGHT, dtype=jnp.int32)
    matched = jnp.sum(named, axis=1)
    token_weight = jnp.sum(jnp.where(named, route_weight[:, :, None], 0.0), axis=1)
    position = jnp.cumsum(matched, axis=0) - 1
    selector = (matched.T[:, None, None, :] == 1) & (
        position.T[:, None, None, :] == jnp.arange(CAP, dtype=jnp.int32)[None, None, :, None]
    )
    selector = jnp.broadcast_to(selector, (FLIGHT, QUARTERS, CAP, tokens))
    which = jnp.arange(QUARTERS)[None, :, None, None]
    sel64 = selector.astype(F32).reshape(-1, tokens)
    wy64 = jnp.where(selector, token_weight.T[:, None, None, :], 0.0).reshape(-1, tokens)
    slot_weight = jnp.sum(wy64, axis=1, keepdims=True)

    def choose(block):
        total = 0.0
        for q in range(QUARTERS):
            picks = (selector & (which == q)).astype(BF16).reshape(-1, tokens)
            total += jnp.dot(
                picks, block[:, q * quarter : (q + 1) * quarter], preferred_element_type=F32
            )
        return total

    send_rows = choose(tokens_in).astype(BF16).reshape(FLIGHT, SLOTS, quarter)
    send_grads = (slot_weight * choose(grads_in)).astype(BF16).reshape(FLIGHT, SLOTS, quarter)

    vmem = pl.BlockSpec(memory_space=pltpu.VMEM)
    hbm = pl.BlockSpec(memory_space=pl.ANY)
    blocks = FLIGHT, SLOTS, quarter
    count = RING * SLOTS
    dma = pltpu.SemaphoreType.DMA
    got_y, got_g, got_wy, got_sel = pl.pallas_call(
        exchange,
        out_shape=(
            jax.ShapeDtypeStruct(blocks, BF16),
            jax.ShapeDtypeStruct(blocks, BF16),
            jax.ShapeDtypeStruct(wy64.shape, F32),
            jax.ShapeDtypeStruct(sel64.shape, F32),
        ),
        in_specs=[vmem] * 4 + [hbm] * 3,
        out_specs=(vmem,) * 4,
        scratch_shapes=[
            pltpu.VMEM(blocks, BF16),
            pltpu.VMEM(blocks, BF16),
            pltpu.VMEM((count, width), BF16),
            pltpu.VMEM((count, width), BF16),
            pltpu.VMEM((width, 4 * units), BF16),
            pltpu.VMEM((2 * units, width), BF16),
            pltpu.VMEM((count, 4 * units), F32),
            pltpu.VMEM((count, 2 * units), F32),
            pltpu.VMEM((count, 2 * units), F32),
            pltpu.VMEM((count, 2 * units), BF16),
            pltpu.VMEM((count, 2 * units), F32),
            pltpu.VMEM((count, 4 * units), BF16),
            pltpu.VMEM((count, width), BF16),
            pltpu.VMEM((count, width), BF16),
            pltpu.VMEM((2, HOPS, SLOTS, half), BF16),
            pltpu.VMEM((2, HOPS, SLOTS, half), BF16),
            pltpu.VMEM(blocks, BF16),
            pltpu.VMEM(blocks, BF16),
            dma((3,)),
            dma((3,)),
            dma((3,)),
            dma((2, FLIGHT)),
            dma((2, FLIGHT)),
            dma((2,)),
            dma((2,)),
            dma((4, 2, HOPS)),
            dma((4, 2, HOPS)),
            dma((2, FLIGHT)),
            dma((2, FLIGHT)),
        ],
        compiler_params=pltpu.CompilerParams(
            collective_id=0, has_side_effects=True, vmem_limit_bytes=48 * 2**20
        ),
        cost_estimate=pl.CostEstimate(
            flops=12 * count * width * units * 2, bytes_accessed=6 * units * width, transcendentals=0
        ),
        name="exchange",
    )(send_rows, send_grads, wy64, sel64, w_gate[0], w_up[0], w_down[0])

    whole = lambda shape: pl.BlockSpec(shape, lambda q: (0,) * len(shape))
    column = pl.BlockSpec((tokens, quarter), lambda q: (0, q))
    passed, grad_passed = pl.pallas_call(
        place_kernel,
        grid=(QUARTERS,),
        out_shape=(jax.ShapeDtypeStruct((tokens, width), BF16),) * 2,
        in_specs=[whole(blocks), whole(blocks), whole(wy64.shape), whole(sel64.shape)],
        out_specs=(column, column),
        name="place",
    )(got_y, got_g, got_wy, got_sel)
    return passed[None], grad_passed[None]


def solution(mesh):
    placed = (
        P("pipe", "expert", None),
        P("pipe", "expert", None),
        P("pipe", "expert", None),
        P("pipe", "expert", None),
        P("pipe", None, "expert"),
        P("pipe", None, "expert"),
        P("pipe", "expert", None),
    )
    return jax.shard_map(
        on_device,
        mesh=mesh,
        in_specs=placed,
        out_specs=(P("pipe", "expert", None), P("pipe", "expert", None)),
        check_vma=False,
    )
```

```python
import jax
import jax.numpy as jnp
from jax import lax
from jax.experimental import pallas as pl
from jax.experimental.pallas import tpu as pltpu
from jax.sharding import PartitionSpec as P

CAP = 4
FLIGHT = 4
QUARTERS = 4
CORES = 2
RING = 8
UNIT = QUARTERS * CAP
STACK = FLIGHT * UNIT
COLS = 256
TILE = 512
MESH = pl.DeviceIdType.MESH
F32 = jnp.float32
BF16 = jnp.bfloat16

RIGHT, LEFT = 0, 1
WAYS = (RIGHT, LEFT)
FROM = {RIGHT: (0, 1, 3, 5, 7), LEFT: (0, 2, 4, 6, 7)}
ROWS = {
    RIGHT: ((0, 0, 1), (0, 1, 1), (0, 2, 1), (0, 3, 1), (1, 0, 2), (1, 2, 2), (2, 0, 2), (2, 2, 2), (3, 0, 2)),
    LEFT: ((0, 0, 1), (0, 3, 1), (0, 2, 1), (0, 1, 1), (1, 2, 2), (1, 0, 2), (2, 2, 2), (2, 0, 2), (3, 2, 2)),
}
GRADS = {
    RIGHT: ((0, 0, 2), (0, 2, 2), (1, 0, 2), (1, 2, 2), (2, 0, 2), (2, 2, 2), (3, 0, 2)),
    LEFT: ((0, 2, 2), (0, 0, 2), (1, 2, 2), (1, 0, 2), (2, 2, 2), (2, 0, 2), (3, 2, 2)),
}
SUMS = {
    LEFT: ((4, 0), (3, 2), (3, 0), (2, 2), (2, 0), (1, 2), (1, 0)),
    RIGHT: ((4, 2), (3, 0), (3, 2), (2, 0), (2, 2), (1, 0), (1, 2)),
}
STEPS = len(SUMS[LEFT])


def nt(left, right):
    return lax.dot_general(left, right, (((1,), (1,)), ((), ())), preferred_element_type=F32)


def tn(left, right):
    return lax.dot_general(left, right, (((0,), (0,)), ((), ())), preferred_element_type=F32)


def dot(left, right):
    return jnp.dot(left, right, preferred_element_type=F32)


def iota(shape, dim):
    return lax.broadcasted_iota(jnp.int32, shape, dim)


def exchange(
    routes_ref, codes_ref, tok_hbm, cot_hbm, wg_ref, wu_ref, wd_ref,
    out_ref, grad_ref,
    tok, cot, pick_x, pick_g, rows, grads, nat, gu, wd, swap, acc, a_gate, a_up, hid, dh, dgu,
    part_y, part_g, recv_y, recv_g, got_y, got_g, sel, wsel, sel_in, wsel_in,
    local_sems, w_send, w_recv, x_send, x_recv, s_send, s_recv,
    ring_send, ring_recv, fin_send, fin_recv,
):
    me = lax.axis_index("expert")
    y = lax.axis_index("pipe")
    pipes = lax.axis_size("pipe")
    core = lax.rem(me, CORES)
    z = lax.rem(lax.div(me, CORES), RING)
    x = lax.div(me, CORES * RING)
    tokens, width = tok.shape
    quarter = width // QUARTERS
    units = wg_ref.shape[1]
    count = nat.shape[0]

    def at(xx, zz, cc, yy):
        return ((xx * RING + zz) * CORES + cc, yy)

    ahead = lax.rem(y + 1, pipes)
    behind = lax.rem(y + pipes - 1, pipes)
    sibling = at(x, z, 1 - core, y)
    next_on = {
        RIGHT: at(x, lax.rem(z + 1, RING), core, y),
        LEFT: at(x, lax.rem(z + RING - 1, RING), core, y),
    }
    plane = [lax.rem(x + k, FLIGHT) for k in range(FLIGHT)]
    across = [at(xx, z, core, y) for xx in plane]
    up = [at(xx, z, core, ahead) for xx in plane]
    down = [at(xx, z, core, behind) for xx in plane]

    barrier = pltpu.get_barrier_semaphore()
    peers = [sibling, next_on[RIGHT], next_on[LEFT]] + across[1:] + up + down
    for peer in peers:
        pl.semaphore_signal(barrier, inc=1, device_id=peer, device_id_type=MESH)

    own = [
        pltpu.make_async_copy(tok_hbm, tok, local_sems.at[0]),
        pltpu.make_async_copy(cot_hbm, cot, local_sems.at[1]),
        pltpu.make_async_copy(wg_ref, gu.at[:, pl.ds(0, units)], local_sems.at[2]),
        pltpu.make_async_copy(wu_ref, gu.at[:, pl.ds(2 * units, units)], local_sems.at[3]),
        pltpu.make_async_copy(wd_ref, wd.at[pl.ds(0, units)], local_sems.at[4]),
    ]
    for copy in own:
        copy.start()

    def remote(src, dst, send, recv, device):
        return pltpu.make_async_remote_copy(
            src_ref=src, dst_ref=dst, send_sem=send, recv_sem=recv,
            device_id=device, device_id_type=MESH,
        )

    routes = routes_ref[...]
    codes = codes_ref[...].astype(F32)
    ratio = 2.5 * codes / jnp.sum(codes, axis=0, keepdims=True)
    named = [routes == f for f in range(FLIGHT)]
    matched = [jnp.sum(jnp.where(hit, 1.0, 0.0), axis=0, keepdims=True) for hit in named]
    weight = [jnp.sum(jnp.where(hit, ratio, 0.0), axis=0, keepdims=True) for hit in named]
    eight = (2 * FLIGHT, tokens)
    stacked = jnp.zeros(eight, F32)
    for f in range(FLIGHT):
        stacked = jnp.where(iota(eight, 0) == f, matched[f], stacked)
    upto = (iota((tokens, tokens), 0) <= iota((tokens, tokens), 1)).astype(F32).astype(BF16)
    rank = dot(stacked.astype(BF16), upto)
    slot = ((iota((UNIT, tokens), 0) & (CAP - 1)) + 1).astype(F32)
    for f in range(FLIGHT):
        here = jnp.where((matched[f] == 1.0) & (rank[f : f + 1] == slot), 1.0, 0.0)
        sel[pl.ds(UNIT * f, UNIT)] = here
        wsel[pl.ds(UNIT * f, UNIT)] = here * weight[f]

    def choose(block, out, scale):
        quarter_of = (iota((STACK, tokens), 0) // CAP) & (QUARTERS - 1)
        picks = [jnp.where(quarter_of == q, sel[...], 0.0).astype(BF16) for q in range(QUARTERS)]
        for i in range(quarter // COLS):
            total = sum(
                dot(picks[q], block[:, q * quarter + i * COLS : q * quarter + (i + 1) * COLS])
                for q in range(QUARTERS)
            )
            if scale is not None:
                total = total * scale
            out[:, :, i * COLS : (i + 1) * COLS] = total.astype(BF16).reshape(FLIGHT, UNIT, COLS)

    def x_copy(i, src, buf, k):
        return remote(
            src.at[plane[k]], buf.at[0, FLIGHT - k], x_send.at[i, k], x_recv.at[i, k], across[k]
        )

    def part_of(buf, place, first, n):
        return buf.at[place, pl.ds(first, n)]

    def gather_copy(kind, buf, order, way, i):
        hops, first, n = order[way][i]
        return remote(
            part_of(buf, FROM[way][hops], first, n), part_of(buf, FROM[way][hops + 1], first, n),
            ring_send.at[kind, way, i], ring_recv.at[kind, way, i], next_on[way],
        )

    arrived = set()

    def arrive(kind, src, buf, order, way, hops, first, n):
        if hops == 0:
            for j in range(max(first, 1), first + n):
                if (kind, j) not in arrived:
                    arrived.add((kind, j))
                    x_copy(kind, src, buf, FLIGHT - j).wait_recv()
            return
        for i, (h, f, m) in enumerate(order[way]):
            if h == hops - 1 and f < first + n and first < f + m and (kind, way, i) not in arrived:
                arrived.add((kind, way, i))
                gather_copy(kind, buf, order, way, i).wait_recv()

    def gather_step(kind, src, buf, order, i):
        for way in WAYS:
            arrive(kind, src, buf, order, way, *order[way][i])
            gather_copy(kind, buf, order, way, i).start()

    def gather_end(kind, src, buf, order):
        for hops in (3, 4):
            for way in WAYS:
                arrive(kind, src, buf, order, way, hops, 0, FLIGHT)

    def sum_copy(kind, part, recv, way, i):
        hops, first = SUMS[way][i]
        return remote(
            part_of(part, FROM[1 - way][hops], first, 2), recv.at[way, i],
            ring_send.at[kind, way, i], ring_recv.at[kind, way, i], next_on[way],
        )

    def sum_step(kind, part, recv, i):
        for way in WAYS:
            hops, first = SUMS[way][i]
            if i >= 2:
                sum_copy(kind, part, recv, way, i - 2).wait_recv()
                at_place = (FROM[1 - way][hops], pl.ds(first, 2))
                part[at_place] = (part[at_place].astype(F32) + recv[way, i - 2].astype(F32)).astype(BF16)
            sum_copy(kind, part, recv, way, i).start()

    def finish(kind, part, recv, got, targets, n):
        copies = []
        for i in (STEPS - 2, STEPS - 1):
            for way in WAYS:
                sum_copy(kind, part, recv, way, i).wait_recv()
        for first in (2, 0):
            came = {way: [i for i in (STEPS - 2, STEPS - 1) if SUMS[way][i][1] == first][0] for way in WAYS}
            at_place = (0, pl.ds(first, 2))
            total = part[at_place].astype(F32) + recv[LEFT, came[LEFT]].astype(F32)
            part[at_place] = (total + recv[RIGHT, came[RIGHT]].astype(F32)).astype(BF16)
            for j in (first, first + 1):
                copy = remote(part.at[0, j], got.at[x], fin_send.at[n, j], fin_recv.at[n, j], targets[j])
                copy.start()
                copies.append(copy)
        return copies

    def regrouping(dim):
        size = (STACK * QUARTERS, STACK * QUARTERS)
        n, m = iota(size, dim), iota(size, 1 - dim)
        low = n & (STACK - 1)
        there = (low // CAP) * UNIT + (n // STACK) * CAP + (low & (CAP - 1))
        return (m == there).astype(F32).astype(BF16)

    def cols_of(i, q=0):
        return pl.ds(pl.multiple_of(q * quarter + i * COLS, COLS), COLS)

    def natural(buf, group):
        def body(i, carry):
            block = buf[pl.ds(4 * group, 4), :, :, cols_of(i)].reshape(STACK * QUARTERS, COLS)
            got = dot(swap[...], block).astype(BF16)
            for q in range(QUARTERS):
                nat[pl.ds(STACK * group, STACK), cols_of(i, q)] = got[q * STACK : (q + 1) * STACK]
            return carry
        lax.fori_loop(0, quarter // COLS, body, 0)

    def blocked(product, part, first, last):
        def body(i, carry):
            pieces = [product(cols_of(i, q)).astype(BF16) for q in range(QUARTERS)]
            for group in range(count // STACK):
                block = jnp.concatenate([p[STACK * group : STACK * (group + 1)] for p in pieces], axis=0)
                got = tn(swap[...], block).astype(BF16)
                part[pl.ds(4 * group, 4), :, :, cols_of(i)] = got.reshape(4, FLIGHT, UNIT, COLS)
            return carry
        lax.fori_loop(first, last, body, 0)

    def gate_up(first, last):
        def body(i, carry):
            ks = pl.ds(pl.multiple_of(i * TILE, TILE), TILE)
            acc[...] += dot(nat[:, ks], gu[ks, :])
            return carry
        lax.fori_loop(first, last, body, 0)

    def activate():
        gate, upper = acc[:, : 2 * units], acc[:, 2 * units :]
        sigma = jax.nn.sigmoid(gate)
        silu = gate * sigma
        hid[...] = (silu * upper).astype(BF16)
        a_gate[...] = upper * sigma * (1.0 + gate * (1.0 - sigma))
        a_up[...] = silu

    def outputs(first, last):
        blocked(lambda cols: dot(hid[...], wd[:, cols]), part_y, first, last)

    def d_hidden(first, last):
        def body(i, carry):
            ks = pl.ds(pl.multiple_of(i * TILE, TILE), TILE)
            dh[...] += nt(nat[:, ks], wd[:, ks])
            return carry
        lax.fori_loop(first, last, body, 0)

    def d_activate():
        dgu[:, : 2 * units] = (dh[...] * a_gate[...]).astype(BF16)
        dgu[:, 2 * units :] = (dh[...] * a_up[...]).astype(BF16)

    def d_inputs(first, last):
        blocked(lambda cols: nt(dgu[...], gu[cols, :]), part_g, first, last)

    def place(weights, got, out):
        terms = weights.shape[1] // STACK
        quarter_of = (iota(weights.shape, 1) // CAP) & (QUARTERS - 1)
        left = jnp.concatenate(
            [jnp.where(quarter_of == q, weights, 0.0).astype(BF16) for q in range(QUARTERS)], axis=0
        )
        def body(i, carry):
            block = got[:, :, cols_of(i)].reshape(STACK, COLS)
            total = dot(left, jnp.concatenate([block] * terms, axis=0)).astype(BF16)
            for q in range(QUARTERS):
                out[:, cols_of(i, q)] = total[q * tokens : (q + 1) * tokens]
            return carry
        lax.fori_loop(0, quarter // COLS, body, 0)

    def three_terms(weights):
        high = weights.astype(BF16).astype(F32)
        mid = (weights - high).astype(BF16).astype(F32)
        low = (weights - high - mid).astype(BF16).astype(F32)
        ends = jnp.concatenate([low, jnp.zeros_like(low)], axis=0).T
        return jnp.concatenate([jnp.concatenate([high, mid], axis=0).T, ends[:, :STACK]], axis=1)

    tiles = width // TILE
    steps = quarter // COLS

    own[0].wait()
    choose(tok, pick_x, None)
    pl.semaphore_wait(barrier, len(peers))
    x_copies = [x_copy(0, pick_x, rows, k) for k in (1, 3, 2)]
    for copy in x_copies:
        copy.start()
    rows[0, 0] = pick_x[x]
    gather_step(0, pick_x, rows, ROWS, 0)
    small = [
        remote(wsel, wsel_in, s_send.at[0], s_recv.at[0], up[0]),
        remote(sel, sel_in, s_send.at[1], s_recv.at[1], down[0]),
    ]
    other = [
        remote(wg_ref, gu.at[:, pl.ds(units, units)], w_send.at[0], w_recv.at[0], sibling),
        remote(wu_ref, gu.at[:, pl.ds(3 * units, units)], w_send.at[1], w_recv.at[1], sibling),
        remote(wd_ref, wd.at[pl.ds(units, units)], w_send.at[2], w_recv.at[2], sibling),
    ]
    for copy in other + small:
        copy.start()
    for i in range(1, 4):
        gather_step(0, pick_x, rows, ROWS, i)
    own[1].wait()
    choose(cot, pick_g, jnp.sum(wsel[...], axis=1, keepdims=True))
    g_copies = [x_copy(1, pick_g, grads, k) for k in (1, 3, 2)]
    for copy in g_copies:
        copy.start()
    grads[0, 0] = pick_g[x]
    gather_step(0, pick_x, rows, ROWS, 4)
    swap[...] = regrouping(0)
    gather_step(0, pick_x, rows, ROWS, 5)
    acc[...] = jnp.zeros_like(acc)
    dh[...] = jnp.zeros_like(dh)
    for i in range(6, len(ROWS[LEFT])):
        gather_step(0, pick_x, rows, ROWS, i)

    gather_step(1, pick_g, grads, GRADS, 0)
    gather_step(1, pick_g, grads, GRADS, 1)
    gather_end(0, pick_x, rows, ROWS)
    natural(rows, 0)
    natural(rows, 1)
    for copy in own[2:]:
        copy.wait()
    for copy in other:
        copy.wait_recv()
    gather_step(1, pick_g, grads, GRADS, 2)
    gate_up(0, tiles // 2)
    gather_step(1, pick_g, grads, GRADS, 3)
    gate_up(tiles // 2, tiles)
    activate()
    gather_step(1, pick_g, grads, GRADS, 4)
    outputs(0, steps // 2)
    gather_step(1, pick_g, grads, GRADS, 5)
    outputs(steps // 2, steps)
    gather_step(1, pick_g, grads, GRADS, 6)

    sum_step(2, part_y, recv_y, 0)
    sum_step(2, part_y, recv_y, 1)
    gather_end(1, pick_g, grads, GRADS)
    natural(grads, 0)
    natural(grads, 1)
    sum_step(2, part_y, recv_y, 2)
    d_hidden(0, tiles)
    d_activate()
    sum_step(2, part_y, recv_y, 3)
    d_inputs(0, steps // 2)
    sum_step(2, part_y, recv_y, 4)
    d_inputs(steps // 2, steps)
    sum_step(2, part_y, recv_y, 5)
    sum_step(2, part_y, recv_y, 6)

    sum_step(3, part_g, recv_g, 0)
    sum_step(3, part_g, recv_g, 1)
    done_y = finish(2, part_y, recv_y, got_y, up, 0)
    sum_step(3, part_g, recv_g, 2)
    small[0].wait_recv()
    weights_y = three_terms(wsel_in[...])
    small[1].wait_recv()
    weights_g = jnp.concatenate([sel_in[...], jnp.zeros_like(sel_in)], axis=0).T[:, :STACK]
    sum_step(3, part_g, recv_g, 3)
    for copy in done_y:
        copy.wait_recv()
    place(weights_y, got_y, out_ref)
    for i in range(4, STEPS):
        sum_step(3, part_g, recv_g, i)
    done_g = finish(3, part_g, recv_g, got_g, down, 1)

    for copy in x_copies + g_copies + other + small + done_y:
        copy.wait_send()
    for way in WAYS:
        for i in range(len(ROWS[way])):
            gather_copy(0, rows, ROWS, way, i).wait_send()
        for i in range(STEPS):
            gather_copy(1, grads, GRADS, way, i).wait_send()
            sum_copy(2, part_y, recv_y, way, i).wait_send()
            sum_copy(3, part_g, recv_g, way, i).wait_send()
    for copy in done_g:
        copy.wait_recv()
    place(weights_g, got_g, grad_ref)
    for copy in done_g:
        copy.wait_send()


def on_device(section_input, cotangent, routes, gate_codes, w_gate, w_up, w_down):
    tokens, width = section_input.shape[1:]
    quarter = width // QUARTERS
    units = w_gate.shape[2]
    count = RING * FLIGHT * CAP
    vmem = pl.BlockSpec(memory_space=pltpu.VMEM)
    hbm = pl.BlockSpec(memory_space=pltpu.HBM)
    dma = pltpu.SemaphoreType.DMA
    blocks = pltpu.VMEM((FLIGHT, UNIT, quarter), BF16)
    gathered = pltpu.VMEM((RING, FLIGHT, UNIT, quarter), BF16)
    incoming = pltpu.VMEM((2, STEPS, 2, UNIT, quarter), BF16)
    block = pltpu.VMEM((tokens, width), BF16)
    half_wide = pltpu.VMEM((count, 2 * units), F32)
    select = pltpu.VMEM((STACK, tokens), F32)
    most = len(ROWS[LEFT])
    passed, grad_passed = pl.pallas_call(
        exchange,
        out_shape=(jax.ShapeDtypeStruct((tokens, width), BF16),) * 2,
        in_specs=[vmem] * 2 + [hbm] * 5,
        out_specs=(vmem,) * 2,
        scratch_shapes=[
            block, block, blocks, blocks, gathered, gathered,
            pltpu.VMEM((count, width), BF16),
            pltpu.VMEM((width, 4 * units), BF16),
            pltpu.VMEM((2 * units, width), BF16),
            pltpu.VMEM((STACK * QUARTERS, STACK * QUARTERS), BF16),
            pltpu.VMEM((count, 4 * units), F32),
            half_wide,
            half_wide,
            pltpu.VMEM((count, 2 * units), BF16),
            half_wide,
            pltpu.VMEM((count, 4 * units), BF16),
            gathered, gathered, incoming, incoming, blocks, blocks,
            select, select, select, select,
            dma((5,)),
            dma((3,)), dma((3,)),
            dma((2, FLIGHT)), dma((2, FLIGHT)),
            dma((2,)), dma((2,)),
            dma((4, 2, most)), dma((4, 2, most)),
            dma((2, FLIGHT)), dma((2, FLIGHT)),
        ],
        compiler_params=pltpu.CompilerParams(
            collective_id=0, has_side_effects=True, vmem_limit_bytes=59 * 2**20
        ),
        cost_estimate=pl.CostEstimate(
            flops=24 * count * width * units, bytes_accessed=14 * tokens * width, transcendentals=0
        ),
        name="exchange",
    )(routes[0].T, gate_codes[0].T, section_input[0], cotangent[0], w_gate[0], w_up[0], w_down[0])
    return passed[None], grad_passed[None]


def solution(mesh):
    placed = (
        P("pipe", "expert", None),
        P("pipe", "expert", None),
        P("pipe", "expert", None),
        P("pipe", "expert", None),
        P("pipe", None, "expert"),
        P("pipe", None, "expert"),
        P("pipe", "expert", None),
    )
    return jax.shard_map(
        on_device,
        mesh=mesh,
        in_specs=placed,
        out_specs=(P("pipe", "expert", None), P("pipe", "expert", None)),
        check_vma=False,
    )
```

```python
import jax
import jax.numpy as jnp
from jax import lax
from jax.experimental import pallas as pl
from jax.experimental.pallas import tpu as pltpu
from jax.sharding import PartitionSpec as P

CAP = 4
FLIGHT = 4
QUARTERS = 4
CORES = 2
RING = 8
UNIT = QUARTERS * CAP
STACK = FLIGHT * UNIT
COLS = 256
TILE = 512
MESH = pl.DeviceIdType.MESH
F32 = jnp.float32
BF16 = jnp.bfloat16

RIGHT, LEFT = 0, 1
WAYS = (RIGHT, LEFT)
FROM = {RIGHT: (0, 1, 3, 5, 7), LEFT: (0, 2, 4, 6, 7)}
ROWS = {
    RIGHT: tuple((hops, j, 1) for hops, order in ((0, (0, 1, 3, 2)), (1, (0, 1, 3, 2)), (2, (0, 1, 3, 2)), (3, (0, 1))) for j in order),
    LEFT: tuple((hops, j, 1) for hops, order in ((0, (0, 3, 1, 2)), (1, (3, 0, 2, 1)), (2, (3, 2, 0, 1)), (3, (3, 2))) for j in order),
}
GRADS = ROWS
LAST = (1, 2, 3, 0)
ENDS = {
    LEFT: tuple((hops, j, 1) for hops, order in ((4, (1, 3)), (3, (2, 0, 1, 3)), (2, (2, 1, 0, 3)), (1, LAST)) for j in order),
    RIGHT: tuple((hops, j, 1) for hops, order in ((4, (2, 0)), (3, (1, 3, 2, 0)), (2, (1, 3, 2, 0)), (1, LAST)) for j in order),
}
OUTS = ENDS
STEPS = len(ENDS[LEFT])
ORDERS = (ROWS, GRADS, OUTS, ENDS)
MOST = max(len(order[way]) for order in ORDERS for way in WAYS)


def nt(left, right):
    return lax.dot_general(left, right, (((1,), (1,)), ((), ())), preferred_element_type=F32)


def tn(left, right):
    return lax.dot_general(left, right, (((0,), (0,)), ((), ())), preferred_element_type=F32)


def dot(left, right):
    return jnp.dot(left, right, preferred_element_type=F32)


def iota(shape, dim):
    return lax.broadcasted_iota(jnp.int32, shape, dim)


def exchange(
    routes_hbm, codes_hbm, tok_hbm, cot_hbm, wg_ref, wu_ref, wd_ref,
    out_hbm, got_g, left_hbm,
    out_ref, left_ref, routes_ref, codes_ref, tok, cot, pick_x, pick_g, rows, grads, nat, gu, wd, swap, acc, a_gate, a_up, hid, dh, dgu,
    part_y, part_g, recv_y, recv_g, got_y, sel, wsel, sel_in, wsel_in,
    local_sems, w_send, w_recv, x_send, x_recv, s_send, s_recv,
    ring_send, ring_recv, fin_send, fin_recv,
):
    me = lax.axis_index("expert")
    y = lax.axis_index("pipe")
    pipes = lax.axis_size("pipe")
    core = lax.rem(me, CORES)
    z = lax.rem(lax.div(me, CORES), RING)
    x = lax.div(me, CORES * RING)
    tokens, width = tok.shape
    quarter = width // QUARTERS
    units = wg_ref.shape[1]
    count = nat.shape[0]

    def at(xx, zz, cc, yy):
        return ((xx * RING + zz) * CORES + cc, yy)

    ahead = lax.rem(y + 1, pipes)
    behind = lax.rem(y + pipes - 1, pipes)
    sibling = at(x, z, 1 - core, y)
    next_on = {
        RIGHT: at(x, lax.rem(z + 1, RING), core, y),
        LEFT: at(x, lax.rem(z + RING - 1, RING), core, y),
    }
    plane = [lax.rem(x + k, FLIGHT) for k in range(FLIGHT)]
    across = [at(xx, z, core, y) for xx in plane]
    up = [at(xx, z, core, ahead) for xx in plane]
    down = [at(xx, z, core, behind) for xx in plane]

    own = [
        pltpu.make_async_copy(routes_hbm, routes_ref, local_sems.at[5]),
        pltpu.make_async_copy(codes_hbm, codes_ref, local_sems.at[6]),
        pltpu.make_async_copy(tok_hbm, tok, local_sems.at[0]),
        pltpu.make_async_copy(cot_hbm, cot, local_sems.at[1]),
        pltpu.make_async_copy(wg_ref, gu.at[:, pl.ds(0, units)], local_sems.at[2]),
        pltpu.make_async_copy(wu_ref, gu.at[:, pl.ds(2 * units, units)], local_sems.at[3]),
        pltpu.make_async_copy(wd_ref, wd.at[pl.ds(0, units)], local_sems.at[4]),
    ]
    for copy in own[:3]:
        copy.start()

    barrier = pltpu.get_barrier_semaphore()
    peers = [sibling, next_on[RIGHT], next_on[LEFT]] + across[1:] + up + down
    for peer in peers:
        pl.semaphore_signal(barrier, inc=1, device_id=peer, device_id_type=MESH)

    def remote(src, dst, send, recv, device):
        return pltpu.make_async_remote_copy(
            src_ref=src, dst_ref=dst, send_sem=send, recv_sem=recv,
            device_id=device, device_id_type=MESH,
        )

    own[0].wait()
    own[1].wait()
    routes = routes_ref[...]
    codes = codes_ref[...].astype(F32)
    ratio = 2.5 * codes / jnp.sum(codes, axis=0, keepdims=True)
    named = [routes == f for f in range(FLIGHT)]
    matched = [jnp.sum(jnp.where(hit, 1.0, 0.0), axis=0, keepdims=True) for hit in named]
    weight = [jnp.sum(jnp.where(hit, ratio, 0.0), axis=0, keepdims=True) for hit in named]
    eight = (2 * FLIGHT, tokens)
    stacked = jnp.zeros(eight, F32)
    for f in range(FLIGHT):
        stacked = jnp.where(iota(eight, 0) == f, matched[f], stacked)
    upto = (iota((tokens, tokens), 0) <= iota((tokens, tokens), 1)).astype(F32).astype(BF16)
    rank = dot(stacked.astype(BF16), upto)
    slot = ((iota((UNIT, tokens), 0) & (CAP - 1)) + 1).astype(F32)
    for f in range(FLIGHT):
        here = jnp.where((matched[f] == 1.0) & (rank[f : f + 1] == slot), 1.0, 0.0)
        sel[pl.ds(UNIT * f, UNIT)] = here
        wsel[pl.ds(UNIT * f, UNIT)] = here * weight[f]

    def choose(block, out, scale, first, last):
        quarter_of = (iota((STACK, tokens), 0) // CAP) & (QUARTERS - 1)
        picks = [jnp.where(quarter_of == q, sel[...], 0.0).astype(BF16) for q in range(QUARTERS)]
        for i in range(first, last):
            total = sum(
                dot(picks[q], block[:, q * quarter + i * COLS : q * quarter + (i + 1) * COLS])
                for q in range(QUARTERS)
            )
            if scale is not None:
                total = total * scale
            out[:, :, i * COLS : (i + 1) * COLS] = total.astype(BF16).reshape(FLIGHT, UNIT, COLS)

    def x_copy(i, src, buf, k):
        return remote(
            src.at[plane[k]], buf.at[0, FLIGHT - k], x_send.at[i, k], x_recv.at[i, k], across[k]
        )

    def part_of(buf, place, first, n):
        return buf.at[place, pl.ds(first, n)]

    def gather_copy(kind, buf, order, way, i):
        hops, first, n = order[way][i]
        return remote(
            part_of(buf, FROM[way][hops], first, n), part_of(buf, FROM[way][hops + 1], first, n),
            ring_send.at[kind, way, i], ring_recv.at[kind, way, i], next_on[way],
        )

    arrived = set()

    def arrive(kind, src, buf, order, way, hops, first, n):
        if hops == 0:
            for j in range(max(first, 1), first + n):
                if (kind, j) not in arrived:
                    arrived.add((kind, j))
                    x_copy(kind, src, buf, FLIGHT - j).wait_recv()
            return
        for i, (h, f, m) in enumerate(order[way]):
            if h == hops - 1 and f < first + n and first < f + m and (kind, way, i) not in arrived:
                arrived.add((kind, way, i))
                gather_copy(kind, buf, order, way, i).wait_recv()

    def gather_step(kind, src, buf, order, i):
        for way in WAYS:
            arrive(kind, src, buf, order, way, *order[way][i])
            gather_copy(kind, buf, order, way, i).start()

    def gather_end(kind, src, buf, order):
        for hops in (3, 4):
            for way in WAYS:
                arrive(kind, src, buf, order, way, hops, 0, FLIGHT)

    def sum_copy(kind, part, recv, way, i):
        hops, first, n = ORDERS[kind][way][i]
        return remote(
            part_of(part, FROM[1 - way][hops], first, n), recv.at[way, hops - 1, pl.ds(first, n)],
            ring_send.at[kind, way, i], ring_recv.at[kind, way, i], next_on[way],
        )

    def sum_arrive(kind, part, recv, way, hops, first, n):
        came = False
        for i, (h, f, m) in enumerate(ORDERS[kind][way]):
            if h == hops + 1 and f < first + n and first < f + m:
                came = True
                if (kind, way, i) not in arrived:
                    arrived.add((kind, way, i))
                    sum_copy(kind, part, recv, way, i).wait_recv()
        return came

    def sum_step(kind, part, recv, i):
        for way in WAYS:
            hops, first, n = ORDERS[kind][way][i]
            if sum_arrive(kind, part, recv, way, hops, first, n):
                here, there = (FROM[1 - way][hops], pl.ds(first, n)), (way, hops, pl.ds(first, n))
                part[here] = (part[here].astype(F32) + recv[there].astype(F32)).astype(BF16)
            sum_copy(kind, part, recv, way, i).start()

    def finish(kind, part, recv, got, targets, order):
        copies = []
        for j in order:
            for way in WAYS:
                sum_arrive(kind, part, recv, way, 0, j, 1)
            total = part[0, j].astype(F32) + recv[LEFT, 0, j].astype(F32)
            part[0, j] = (total + recv[RIGHT, 0, j].astype(F32)).astype(BF16)
            copy = remote(
                part.at[0, j], got.at[x], fin_send.at[kind - 2, j], fin_recv.at[kind - 2, j], targets[j]
            )
            copy.start()
            copies.append(copy)
        return copies

    def regrouping(dim):
        size = (STACK * QUARTERS, STACK * QUARTERS)
        n, m = iota(size, dim), iota(size, 1 - dim)
        low = n & (STACK - 1)
        there = (low // CAP) * UNIT + (n // STACK) * CAP + (low & (CAP - 1))
        return (m == there).astype(F32).astype(BF16)

    def cols_of(i, q=0):
        return pl.ds(pl.multiple_of(q * quarter + i * COLS, COLS), COLS)

    def natural(buf, group):
        def body(i, carry):
            block = buf[pl.ds(4 * group, 4), :, :, cols_of(i)].reshape(STACK * QUARTERS, COLS)
            got = dot(swap[...], block).astype(BF16)
            for q in range(QUARTERS):
                nat[pl.ds(STACK * group, STACK), cols_of(i, q)] = got[q * STACK : (q + 1) * STACK]
            return carry
        lax.fori_loop(0, quarter // COLS, body, 0)

    def blocked(product, part, first, last):
        def body(i, carry):
            pieces = [product(cols_of(i, q)).astype(BF16) for q in range(QUARTERS)]
            for group in range(count // STACK):
                block = jnp.concatenate([p[STACK * group : STACK * (group + 1)] for p in pieces], axis=0)
                got = tn(swap[...], block).astype(BF16)
                part[pl.ds(4 * group, 4), :, :, cols_of(i)] = got.reshape(4, FLIGHT, UNIT, COLS)
            return carry
        lax.fori_loop(first, last, body, 0)

    def gate_up(first, last):
        def body(i, carry):
            ks = pl.ds(pl.multiple_of(i * TILE, TILE), TILE)
            acc[...] += dot(nat[:, ks], gu[ks, :])
            return carry
        lax.fori_loop(first, last, body, 0)

    def activate():
        gate, upper = acc[:, : 2 * units], acc[:, 2 * units :]
        sigma = jax.nn.sigmoid(gate)
        silu = gate * sigma
        hid[...] = (silu * upper).astype(BF16)
        a_gate[...] = upper * sigma * (1.0 + gate * (1.0 - sigma))
        a_up[...] = silu

    def outputs(first, last):
        blocked(lambda cols: dot(hid[...], wd[:, cols]), part_y, first, last)

    def d_hidden(first, last):
        def body(i, carry):
            ks = pl.ds(pl.multiple_of(i * TILE, TILE), TILE)
            dh[...] += nt(nat[:, ks], wd[:, ks])
            return carry
        lax.fori_loop(first, last, body, 0)

    def d_activate():
        dgu[:, : 2 * units] = (dh[...] * a_gate[...]).astype(BF16)
        dgu[:, 2 * units :] = (dh[...] * a_up[...]).astype(BF16)

    def d_inputs(first, last):
        blocked(lambda cols: nt(dgu[...], gu[cols, :]), part_g, first, last)

    def by_quarter(weights):
        quarter_of = (iota(weights.shape, 1) // CAP) & (QUARTERS - 1)
        return jnp.concatenate(
            [jnp.where(quarter_of == q, weights, 0.0).astype(BF16) for q in range(QUARTERS)], axis=0
        )

    def place(left, got, out):
        terms = left.shape[1] // STACK
        def body(i, carry):
            block = got[:, :, cols_of(i)].reshape(STACK, COLS)
            total = dot(left, jnp.concatenate([block] * terms, axis=0)).astype(BF16)
            for q in range(QUARTERS):
                out[:, cols_of(i, q)] = total[q * tokens : (q + 1) * tokens]
            return carry
        lax.fori_loop(0, quarter // COLS, body, 0)

    def three_terms(weights):
        high = weights.astype(BF16).astype(F32)
        mid = (weights - high).astype(BF16).astype(F32)
        low = (weights - high - mid).astype(BF16).astype(F32)
        ends = jnp.concatenate([low, jnp.zeros_like(low)], axis=0).T
        return jnp.concatenate([jnp.concatenate([high, mid], axis=0).T, ends[:, :STACK]], axis=1)

    tiles = width // TILE
    steps = quarter // COLS

    own[2].wait()
    own[3].start()
    choose(tok, pick_x, None, 0, steps)
    pl.semaphore_wait(barrier, len(peers))
    x_copies = [x_copy(0, pick_x, rows, k) for k in (1, 3, 2)]
    for copy in x_copies:
        copy.start()
    rows[0, 0] = pick_x[x]
    def row_steps(*which):
        for i in which:
            gather_step(0, pick_x, rows, ROWS, i)

    def grad_steps(*which):
        for i in which:
            gather_step(1, pick_g, grads, GRADS, i)

    def out_steps(*which):
        for i in which:
            sum_step(2, part_y, recv_y, i)

    def end_steps(*which):
        for i in which:
            sum_step(3, part_g, recv_g, i)

    row_steps(0)
    own[3].wait()
    for copy in own[4:]:
        copy.start()
    choose(cot, pick_g, jnp.sum(wsel[...], axis=1, keepdims=True), 0, steps)
    g_copies = [x_copy(1, pick_g, grads, k) for k in (1, 3, 2)]
    for copy in g_copies:
        copy.start()
    grads[0, 0] = pick_g[x]
    grad_steps(0)
    row_steps(1, 2)
    grad_steps(1, 2)
    row_steps(3, 4)
    small = [
        remote(wsel, wsel_in, s_send.at[0], s_recv.at[0], up[0]),
        remote(sel, sel_in, s_send.at[1], s_recv.at[1], down[0]),
    ]
    other = [
        remote(wg_ref, gu.at[:, pl.ds(units, units)], w_send.at[0], w_recv.at[0], sibling),
        remote(wu_ref, gu.at[:, pl.ds(3 * units, units)], w_send.at[1], w_recv.at[1], sibling),
        remote(wd_ref, wd.at[pl.ds(units, units)], w_send.at[2], w_recv.at[2], sibling),
    ]
    for copy in other + small:
        copy.start()
    row_steps(5, 6)
    swap[...] = regrouping(0)
    row_steps(7, 8)
    acc[...] = jnp.zeros_like(acc)
    dh[...] = jnp.zeros_like(dh)
    row_steps(9, 10, 11, 12, 13)
    grad_steps(3, 4)
    arrive(0, pick_x, rows, ROWS, RIGHT, 2, 0, FLIGHT)
    natural(rows, 0)
    grad_steps(5)

    gather_end(0, pick_x, rows, ROWS)
    natural(rows, 1)
    for copy in own[4:]:
        copy.wait()
    for copy in other:
        copy.wait_recv()
    grad_steps(6)
    gate_up(0, tiles // 2)
    grad_steps(7, 8)
    gate_up(tiles // 2, tiles)
    activate()
    grad_steps(9, 10)
    outputs(0, 2)
    grad_steps(11)
    outputs(2, 4)
    grad_steps(12)
    outputs(4, 6)
    grad_steps(13)
    outputs(6, steps)

    out_steps(0, 1)
    arrive(1, pick_g, grads, GRADS, RIGHT, 2, 0, FLIGHT)
    natural(grads, 0)
    out_steps(2)
    gather_end(1, pick_g, grads, GRADS)
    natural(grads, 1)
    out_steps(3)
    d_hidden(0, tiles)
    d_activate()
    out_steps(4, 5)
    d_inputs(0, 2)
    out_steps(6, 7)
    d_inputs(2, 4)
    out_steps(8, 9)
    d_inputs(4, 6)
    out_steps(10, 11)
    d_inputs(6, steps)
    out_steps(12)
    end_steps(0, 1)
    out_steps(13)
    end_steps(2, 3)

    done_y = finish(2, part_y, recv_y, got_y, up, LAST)
    end_steps(4, 5)
    small[0].wait_recv()
    weights_y = by_quarter(three_terms(wsel_in[...]))
    small[1].wait_recv()
    left_ref[...] = by_quarter(jnp.concatenate([sel_in[...], jnp.zeros_like(sel_in)], axis=0).T[:, :STACK])
    end_steps(6, 7)
    for copy in done_y:
        copy.wait_recv()
    place(weights_y, got_y, out_ref)
    results = [
        pltpu.make_async_copy(out_ref, out_hbm, local_sems.at[7]),
        pltpu.make_async_copy(left_ref, left_hbm, local_sems.at[8]),
    ]
    for copy in results:
        copy.start()
    end_steps(8, 9)
    for copy in x_copies + g_copies + other + small + done_y:
        copy.wait_send()
    end_steps(10, 11, 12, 13)
    for i in range(STEPS):
        for way in WAYS:
            gather_copy(0, rows, ROWS, way, i).wait_send()
            gather_copy(1, grads, GRADS, way, i).wait_send()
            sum_copy(2, part_y, recv_y, way, i).wait_send()
    done_g = finish(3, part_g, recv_g, got_g, down, LAST)
    for i in range(STEPS):
        for way in WAYS:
            sum_copy(3, part_g, recv_g, way, i).wait_send()
    for copy in done_g + results:
        copy.wait()


def write_out(y_hbm, g_hbm, left_hbm, out_hbm, grad_hbm, y_ref, g_ref, left_ref, dense, in_sems, y_sems, sems):
    tokens, width = y_hbm.shape
    quarter = width // QUARTERS
    needed = [
        pltpu.make_async_copy(g_hbm, g_ref, in_sems.at[0]),
        pltpu.make_async_copy(left_hbm, left_ref, in_sems.at[1]),
    ]
    for copy in needed:
        copy.start()
    part = tokens // QUARTERS
    here = []
    for n in range(QUARTERS):
        rows = pl.ds(n * part, part)
        here.append(pltpu.make_async_copy(y_hbm.at[rows], y_ref.at[rows], in_sems.at[2 + n]))
        here[n].start()
    for copy in needed:
        copy.wait()
    left = left_ref[...]
    copies = []
    for n in range(QUARTERS):
        rows = pl.ds(n * part, part)
        here[n].wait()
        copies.append(pltpu.make_async_copy(y_ref.at[rows], out_hbm.at[rows], y_sems.at[n]))
        copies[n].start()
    cuts = (0, 3, 5, 7)
    for n in range(len(cuts) - 1):
        for i in range(cuts[n], cuts[n + 1]):
            block = g_ref[:, :, i * COLS : (i + 1) * COLS].reshape(STACK, COLS)
            total = dot(left, block).astype(BF16)
            for q in range(QUARTERS):
                dense[:, q * quarter + i * COLS : q * quarter + (i + 1) * COLS] = total[q * tokens : (q + 1) * tokens]
        for q in range(QUARTERS):
            cols = pl.ds(q * quarter + cuts[n] * COLS, (cuts[n + 1] - cuts[n]) * COLS)
            copy = pltpu.make_async_copy(
                dense.at[:, cols], grad_hbm.at[:, cols], sems.at[n * QUARTERS + q]
            )
            copy.start()
            copies.append(copy)
    for copy in copies:
        copy.wait()


def on_device(section_input, cotangent, routes, gate_codes, w_gate, w_up, w_down):
    tokens, width = section_input.shape[1:]
    quarter = width // QUARTERS
    units = w_gate.shape[2]
    count = RING * FLIGHT * CAP
    hbm = pl.BlockSpec(memory_space=pltpu.HBM)
    dma = pltpu.SemaphoreType.DMA
    blocks = pltpu.VMEM((FLIGHT, UNIT, quarter), BF16)
    gathered = pltpu.VMEM((RING, FLIGHT, UNIT, quarter), BF16)
    incoming = pltpu.VMEM((2, 4, FLIGHT, UNIT, quarter), BF16)
    block = pltpu.VMEM((tokens, width), BF16)
    route = pltpu.VMEM(routes.shape[:0:-1], jnp.int32)
    half_wide = pltpu.VMEM((count, 2 * units), F32)
    select = pltpu.VMEM((STACK, tokens), F32)
    dense = jax.ShapeDtypeStruct((tokens, width), BF16)
    out_dense, got_g, left = pl.pallas_call(
        exchange,
        out_shape=(
            dense,
            jax.ShapeDtypeStruct((FLIGHT, UNIT, quarter), BF16),
            jax.ShapeDtypeStruct((QUARTERS * tokens, STACK), BF16),
        ),
        in_specs=[hbm] * 7,
        out_specs=(hbm,) * 3,
        scratch_shapes=[
            block, pltpu.VMEM((QUARTERS * tokens, STACK), BF16), route, route, block, block, blocks, blocks, gathered, gathered,
            pltpu.VMEM((count, width), BF16),
            pltpu.VMEM((width, 4 * units), BF16),
            pltpu.VMEM((2 * units, width), BF16),
            pltpu.VMEM((STACK * QUARTERS, STACK * QUARTERS), BF16),
            pltpu.VMEM((count, 4 * units), F32),
            half_wide,
            half_wide,
            pltpu.VMEM((count, 2 * units), BF16),
            half_wide,
            pltpu.VMEM((count, 4 * units), BF16),
            gathered, gathered, incoming, incoming, blocks,
            select, select, select, select,
            dma((9,)),
            dma((3,)), dma((3,)),
            dma((2, FLIGHT)), dma((2, FLIGHT)),
            dma((2,)), dma((2,)),
            dma((4, 2, MOST)), dma((4, 2, MOST)),
            dma((2, FLIGHT)), dma((2, FLIGHT)),
        ],
        compiler_params=pltpu.CompilerParams(
            collective_id=0, has_side_effects=True, vmem_limit_bytes=57 * 2**20
        ),
        cost_estimate=pl.CostEstimate(
            flops=24 * count * width * units, bytes_accessed=14 * tokens * width, transcendentals=0
        ),
        name="exchange",
    )(routes[0].T, gate_codes[0].T, section_input[0], cotangent[0], w_gate[0], w_up[0], w_down[0])
    passed, grad_passed = pl.pallas_call(
        write_out,
        out_shape=(dense,) * 2,
        in_specs=[hbm] * 3,
        out_specs=(hbm,) * 2,
        scratch_shapes=[
            block, blocks, pltpu.VMEM((QUARTERS * tokens, STACK), BF16), block,
            dma((2 + QUARTERS,)), dma((QUARTERS,)), dma((3 * QUARTERS,)),
        ],
        compiler_params=pltpu.CompilerParams(vmem_limit_bytes=57 * 2**20),
        name="write_out",
    )(out_dense, got_g, left)
    return passed[None], grad_passed[None]


def solution(mesh):
    placed = (
        P("pipe", "expert", None),
        P("pipe", "expert", None),
        P("pipe", "expert", None),
        P("pipe", "expert", None),
        P("pipe", None, "expert"),
        P("pipe", None, "expert"),
        P("pipe", "expert", None),
    )
    return jax.shard_map(
        on_device,
        mesh=mesh,
        in_specs=placed,
        out_specs=(P("pipe", "expert", None), P("pipe", "expert", None)),
        check_vma=False,
    )
```

```python
import jax
import jax.numpy as jnp
from jax import lax
from jax.experimental import pallas as pl
from jax.experimental.pallas import tpu as pltpu
from jax.sharding import PartitionSpec as P

CAP = 4
FLIGHT = 4
QUARTERS = 4
CORES = 2
RING = 8
UNIT = QUARTERS * CAP
STACK = FLIGHT * UNIT
COLS = 256
TILE = 512
MESH = pl.DeviceIdType.MESH
F32 = jnp.float32
BF16 = jnp.bfloat16

RIGHT, LEFT = 0, 1
WAYS = (RIGHT, LEFT)
FROM = {RIGHT: (0, 1, 3, 5, 7), LEFT: (0, 2, 4, 6, 7)}
ROWS = {
    RIGHT: tuple((hops, j, 1) for hops, order in ((0, (0, 1, 3, 2)), (1, (0, 1, 3, 2)), (2, (0, 1, 3, 2)), (3, (0, 1))) for j in order),
    LEFT: tuple((hops, j, 1) for hops, order in ((0, (0, 3, 1, 2)), (1, (3, 0, 2, 1)), (2, (3, 2, 0, 1)), (3, (3, 2))) for j in order),
}
GRADS = {
    RIGHT: ROWS[RIGHT],
    LEFT: tuple((hops, j, 1) for hops, order in ((0, (0, 3, 2, 1)), (1, (3, 2, 0, 1)), (2, (3, 2, 0, 1)), (3, (3, 2))) for j in order),
}
LAST = (1, 2, 3, 0)
ENDS = {
    LEFT: tuple((hops, j, 1) for hops, order in ((4, (1, 3)), (3, (2, 0, 1, 3)), (2, (2, 1, 0, 3)), (1, LAST)) for j in order),
    RIGHT: tuple((hops, j, 1) for hops, order in ((4, (2, 0)), (3, (1, 3, 2, 0)), (2, (1, 3, 2, 0)), (1, LAST)) for j in order),
}
OUTS = {
    LEFT: tuple((hops, j, 1) for hops, order in ((4, (1, 3)), (3, (2, 0, 1, 3)), (2, (2, 0, 1, 3)), (1, (2, 0, 1, 3))) for j in order),
    RIGHT: tuple((hops, j, 1) for hops, order in ((4, (2, 0)), (3, (1, 3, 2, 0)), (2, (1, 3, 2, 0)), (1, (1, 3, 2, 0))) for j in order),
}
STEPS = len(ENDS[LEFT])
ORDERS = (ROWS, GRADS, OUTS, ENDS)
MOST = max(len(order[way]) for order in ORDERS for way in WAYS)


def nt(left, right):
    return lax.dot_general(left, right, (((1,), (1,)), ((), ())), preferred_element_type=F32)


def tn(left, right):
    return lax.dot_general(left, right, (((0,), (0,)), ((), ())), preferred_element_type=F32)


def dot(left, right):
    return jnp.dot(left, right, preferred_element_type=F32)


def iota(shape, dim):
    return lax.broadcasted_iota(jnp.int32, shape, dim)


def exchange(
    routes_hbm, codes_hbm, tok_hbm, cot_hbm, wg_ref, wu_ref, wd_ref,
    out_hbm, got_g, left_hbm,
    out_ref, left_ref, routes_ref, codes_ref, tok, cot, pick_x, pick_g, rows, grads, nat, gu, wd, swap, acc, a_gate, a_up, hid, dh, dgu,
    part_y, part_g, recv_y, recv_g, got_y, sel, wsel, sel_in, wsel_in,
    local_sems, w_send, w_recv, x_send, x_recv, s_send, s_recv,
    ring_send, ring_recv, fin_send, fin_recv,
):
    me = lax.axis_index("expert")
    y = lax.axis_index("pipe")
    pipes = lax.axis_size("pipe")
    core = lax.rem(me, CORES)
    z = lax.rem(lax.div(me, CORES), RING)
    x = lax.div(me, CORES * RING)
    tokens, width = tok.shape
    quarter = width // QUARTERS
    units = wg_ref.shape[1]
    count = nat.shape[0]

    def at(xx, zz, cc, yy):
        return ((xx * RING + zz) * CORES + cc, yy)

    ahead = lax.rem(y + 1, pipes)
    behind = lax.rem(y + pipes - 1, pipes)
    sibling = at(x, z, 1 - core, y)
    next_on = {
        RIGHT: at(x, lax.rem(z + 1, RING), core, y),
        LEFT: at(x, lax.rem(z + RING - 1, RING), core, y),
    }
    plane = [lax.rem(x + k, FLIGHT) for k in range(FLIGHT)]
    across = [at(xx, z, core, y) for xx in plane]
    up = [at(xx, z, core, ahead) for xx in plane]
    down = [at(xx, z, core, behind) for xx in plane]

    own = [
        pltpu.make_async_copy(routes_hbm, routes_ref, local_sems.at[5]),
        pltpu.make_async_copy(codes_hbm, codes_ref, local_sems.at[6]),
        pltpu.make_async_copy(tok_hbm, tok, local_sems.at[0]),
        pltpu.make_async_copy(cot_hbm, cot, local_sems.at[1]),
        pltpu.make_async_copy(wg_ref, gu.at[:, pl.ds(0, units)], local_sems.at[2]),
        pltpu.make_async_copy(wu_ref, gu.at[:, pl.ds(2 * units, units)], local_sems.at[3]),
        pltpu.make_async_copy(wd_ref, wd.at[pl.ds(0, units)], local_sems.at[4]),
    ]
    for copy in own[:3]:
        copy.start()

    barrier = pltpu.get_barrier_semaphore()
    peers = [sibling, next_on[RIGHT], next_on[LEFT]] + across[1:] + up + down
    for peer in peers:
        pl.semaphore_signal(barrier, inc=1, device_id=peer, device_id_type=MESH)

    def remote(src, dst, send, recv, device):
        return pltpu.make_async_remote_copy(
            src_ref=src, dst_ref=dst, send_sem=send, recv_sem=recv,
            device_id=device, device_id_type=MESH,
        )

    own[0].wait()
    own[1].wait()
    routes = routes_ref[...]
    codes = codes_ref[...].astype(F32)
    ratio = 2.5 * codes / jnp.sum(codes, axis=0, keepdims=True)
    named = [routes == f for f in range(FLIGHT)]
    matched = [jnp.sum(jnp.where(hit, 1.0, 0.0), axis=0, keepdims=True) for hit in named]
    weight = [jnp.sum(jnp.where(hit, ratio, 0.0), axis=0, keepdims=True) for hit in named]
    eight = (2 * FLIGHT, tokens)
    stacked = jnp.zeros(eight, F32)
    for f in range(FLIGHT):
        stacked = jnp.where(iota(eight, 0) == f, matched[f], stacked)
    upto = (iota((tokens, tokens), 0) <= iota((tokens, tokens), 1)).astype(F32).astype(BF16)
    rank = dot(stacked.astype(BF16), upto)
    slot = ((iota((UNIT, tokens), 0) & (CAP - 1)) + 1).astype(F32)
    for f in range(FLIGHT):
        here = jnp.where((matched[f] == 1.0) & (rank[f : f + 1] == slot), 1.0, 0.0)
        sel[pl.ds(UNIT * f, UNIT)] = here
        wsel[pl.ds(UNIT * f, UNIT)] = here * weight[f]

    def choose(block, out, scale, first, last):
        quarter_of = (iota((STACK, tokens), 0) // CAP) & (QUARTERS - 1)
        picks = [jnp.where(quarter_of == q, sel[...], 0.0).astype(BF16) for q in range(QUARTERS)]
        for i in range(first, last):
            total = sum(
                dot(picks[q], block[:, q * quarter + i * COLS : q * quarter + (i + 1) * COLS])
                for q in range(QUARTERS)
            )
            if scale is not None:
                total = total * scale
            out[:, :, i * COLS : (i + 1) * COLS] = total.astype(BF16).reshape(FLIGHT, UNIT, COLS)

    def x_copy(i, src, buf, k):
        return remote(
            src.at[plane[k]], buf.at[0, FLIGHT - k], x_send.at[i, k], x_recv.at[i, k], across[k]
        )

    def part_of(buf, place, first, n):
        return buf.at[place, pl.ds(first, n)]

    def gather_copy(kind, buf, order, way, i):
        hops, first, n = order[way][i]
        return remote(
            part_of(buf, FROM[way][hops], first, n), part_of(buf, FROM[way][hops + 1], first, n),
            ring_send.at[kind, way, i], ring_recv.at[kind, way, i], next_on[way],
        )

    arrived = set()

    def arrive(kind, src, buf, order, way, hops, first, n):
        if hops == 0:
            for j in range(max(first, 1), first + n):
                if (kind, j) not in arrived:
                    arrived.add((kind, j))
                    x_copy(kind, src, buf, FLIGHT - j).wait_recv()
            return
        for i, (h, f, m) in enumerate(order[way]):
            if h == hops - 1 and f < first + n and first < f + m and (kind, way, i) not in arrived:
                arrived.add((kind, way, i))
                gather_copy(kind, buf, order, way, i).wait_recv()

    def gather_step(kind, src, buf, order, i):
        for way in WAYS:
            arrive(kind, src, buf, order, way, *order[way][i])
            gather_copy(kind, buf, order, way, i).start()

    def gather_end(kind, src, buf, order):
        for hops in (3, 4):
            for way in WAYS:
                arrive(kind, src, buf, order, way, hops, 0, FLIGHT)

    def sum_copy(kind, part, recv, way, i):
        hops, first, n = ORDERS[kind][way][i]
        return remote(
            part_of(part, FROM[1 - way][hops], first, n), recv.at[way, hops - 1, pl.ds(first, n)],
            ring_send.at[kind, way, i], ring_recv.at[kind, way, i], next_on[way],
        )

    def sum_arrive(kind, part, recv, way, hops, first, n):
        came = False
        for i, (h, f, m) in enumerate(ORDERS[kind][way]):
            if h == hops + 1 and f < first + n and first < f + m:
                came = True
                if (kind, way, i) not in arrived:
                    arrived.add((kind, way, i))
                    sum_copy(kind, part, recv, way, i).wait_recv()
        return came

    def sum_step(kind, part, recv, i):
        for way in WAYS:
            hops, first, n = ORDERS[kind][way][i]
            if sum_arrive(kind, part, recv, way, hops, first, n):
                here, there = (FROM[1 - way][hops], pl.ds(first, n)), (way, hops, pl.ds(first, n))
                part[here] = (part[here].astype(F32) + recv[there].astype(F32)).astype(BF16)
            sum_copy(kind, part, recv, way, i).start()

    def finish(kind, part, recv, got, targets, order):
        copies = []
        for j in order:
            for way in WAYS:
                sum_arrive(kind, part, recv, way, 0, j, 1)
            total = part[0, j].astype(F32) + recv[LEFT, 0, j].astype(F32)
            part[0, j] = (total + recv[RIGHT, 0, j].astype(F32)).astype(BF16)
            copy = remote(
                part.at[0, j], got.at[x], fin_send.at[kind - 2, j], fin_recv.at[kind - 2, j], targets[j]
            )
            copy.start()
            copies.append(copy)
        return copies

    def regrouping(dim):
        size = (STACK * QUARTERS, STACK * QUARTERS)
        n, m = iota(size, dim), iota(size, 1 - dim)
        low = n & (STACK - 1)
        there = (low // CAP) * UNIT + (n // STACK) * CAP + (low & (CAP - 1))
        return (m == there).astype(F32).astype(BF16)

    def cols_of(i, q=0):
        start = q * quarter + i * COLS
        return pl.ds(start if isinstance(start, int) else pl.multiple_of(start, COLS), COLS)

    def natural(buf, group):
        for i in range(quarter // COLS):
            block = buf[pl.ds(4 * group, 4), :, :, cols_of(i)].reshape(STACK * QUARTERS, COLS)
            got = dot(swap[...], block).astype(BF16)
            for q in range(QUARTERS):
                nat[pl.ds(STACK * group, STACK), cols_of(i, q)] = got[q * STACK : (q + 1) * STACK]

    def blocked(product, part, first, last):
        for i in range(first, last):
            pieces = [product(cols_of(i, q)).astype(BF16) for q in range(QUARTERS)]
            for group in range(count // STACK):
                block = jnp.concatenate([p[STACK * group : STACK * (group + 1)] for p in pieces], axis=0)
                got = tn(swap[...], block).astype(BF16)
                part[pl.ds(4 * group, 4), :, :, cols_of(i)] = got.reshape(4, FLIGHT, UNIT, COLS)

    def gate_up(first, last):
        ks = pl.ds(first * TILE, (last - first) * TILE)
        for n in range(0, 4 * units, COLS):
            cols = pl.ds(n, COLS)
            acc[:, cols] += dot(nat[:, ks], gu[ks, cols])

    def activate():
        gate, upper = acc[:, : 2 * units], acc[:, 2 * units :]
        sigma = jax.nn.sigmoid(gate)
        silu = gate * sigma
        hid[...] = (silu * upper).astype(BF16)
        a_gate[...] = upper * sigma * (1.0 + gate * (1.0 - sigma))
        a_up[...] = silu

    def outputs(first, last):
        blocked(lambda cols: dot(hid[...], wd[:, cols]), part_y, first, last)

    def d_hidden(first, last):
        ks = pl.ds(first * TILE, (last - first) * TILE)
        dh[...] += nt(nat[:, ks], wd[:, ks])

    def d_activate():
        dgu[:, : 2 * units] = (dh[...] * a_gate[...]).astype(BF16)
        dgu[:, 2 * units :] = (dh[...] * a_up[...]).astype(BF16)

    def d_inputs(first, last):
        blocked(lambda cols: nt(dgu[...], gu[cols, :]), part_g, first, last)

    def by_quarter(weights):
        quarter_of = (iota(weights.shape, 1) // CAP) & (QUARTERS - 1)
        return jnp.concatenate(
            [jnp.where(quarter_of == q, weights, 0.0).astype(BF16) for q in range(QUARTERS)], axis=0
        )

    def place(left, got, out):
        terms = left.shape[1] // STACK
        for i in range(quarter // COLS):
            block = got[:, :, cols_of(i)].reshape(STACK, COLS)
            total = dot(left, jnp.concatenate([block] * terms, axis=0)).astype(BF16)
            for q in range(QUARTERS):
                out[:, cols_of(i, q)] = total[q * tokens : (q + 1) * tokens]

    def three_terms(weights):
        high = weights.astype(BF16).astype(F32)
        mid = (weights - high).astype(BF16).astype(F32)
        low = (weights - high - mid).astype(BF16).astype(F32)
        ends = jnp.concatenate([low, jnp.zeros_like(low)], axis=0).T
        return jnp.concatenate([jnp.concatenate([high, mid], axis=0).T, ends[:, :STACK]], axis=1)

    tiles = width // TILE
    steps = quarter // COLS

    own[2].wait()
    own[3].start()
    choose(tok, pick_x, None, 0, steps)
    pl.semaphore_wait(barrier, len(peers))
    x_copies = [x_copy(0, pick_x, rows, k) for k in (1, 3, 2)]
    for copy in x_copies:
        copy.start()
    rows[0, 0] = pick_x[x]
    def row_steps(*which):
        for i in which:
            gather_step(0, pick_x, rows, ROWS, i)

    def grad_steps(*which):
        for i in which:
            gather_step(1, pick_g, grads, GRADS, i)

    def out_steps(*which):
        for i in which:
            sum_step(2, part_y, recv_y, i)

    def end_steps(*which):
        for i in which:
            sum_step(3, part_g, recv_g, i)

    row_steps(0)
    own[3].wait()
    for copy in own[4:]:
        copy.start()
    choose(cot, pick_g, jnp.sum(wsel[...], axis=1, keepdims=True), 0, steps)
    g_copies = [x_copy(1, pick_g, grads, k) for k in (1, 3, 2)]
    for copy in g_copies:
        copy.start()
    grads[0, 0] = pick_g[x]
    grad_steps(0)
    row_steps(1, 2)
    grad_steps(1, 2)
    row_steps(3, 4)
    small = [
        remote(wsel, wsel_in, s_send.at[0], s_recv.at[0], up[0]),
        remote(sel, sel_in, s_send.at[1], s_recv.at[1], down[0]),
    ]
    other = [
        remote(wg_ref, gu.at[:, pl.ds(units, units)], w_send.at[0], w_recv.at[0], sibling),
        remote(wu_ref, gu.at[:, pl.ds(3 * units, units)], w_send.at[1], w_recv.at[1], sibling),
        remote(wd_ref, wd.at[pl.ds(units, units)], w_send.at[2], w_recv.at[2], sibling),
    ]
    for copy in other + small:
        copy.start()
    row_steps(5, 6)
    swap[...] = regrouping(0)
    row_steps(7, 8)
    acc[...] = jnp.zeros_like(acc)
    dh[...] = jnp.zeros_like(dh)
    row_steps(9, 10, 11, 12, 13)
    grad_steps(3, 4)
    arrive(0, pick_x, rows, ROWS, RIGHT, 2, 0, FLIGHT)
    natural(rows, 0)
    grad_steps(5)

    gather_end(0, pick_x, rows, ROWS)
    natural(rows, 1)
    for copy in own[4:]:
        copy.wait()
    for copy in other:
        copy.wait_recv()
    grad_steps(6)
    gate_up(0, tiles // 2)
    grad_steps(7, 8)
    gate_up(tiles // 2, tiles)
    activate()
    grad_steps(9, 10)
    outputs(0, 2)
    grad_steps(11)
    outputs(2, 4)
    grad_steps(12)
    outputs(4, 6)
    grad_steps(13)
    outputs(6, steps)

    out_steps(0, 1)
    arrive(1, pick_g, grads, GRADS, RIGHT, 2, 0, FLIGHT)
    natural(grads, 0)
    out_steps(2)
    gather_end(1, pick_g, grads, GRADS)
    natural(grads, 1)
    out_steps(3)
    d_hidden(0, tiles)
    d_activate()
    out_steps(4, 5)
    d_inputs(0, 2)
    out_steps(6, 7)
    d_inputs(2, 4)
    out_steps(8)
    d_inputs(4, 6)
    out_steps(9)
    d_inputs(6, steps)
    end_steps(0, 1)
    out_steps(10)
    end_steps(2, 3)
    small[0].wait_recv()
    weights_y = by_quarter(three_terms(wsel_in[...]))
    small[1].wait_recv()
    left_ref[...] = by_quarter(jnp.concatenate([sel_in[...], jnp.zeros_like(sel_in)], axis=0).T[:, :STACK])
    out_steps(11)
    end_steps(4, 5)
    for copy in x_copies + g_copies + other + small:
        copy.wait_send()
    out_steps(12)
    end_steps(6, 7)
    out_steps(13)
    end_steps(8, 9, 10)
    for i in range(STEPS):
        for way in WAYS:
            gather_copy(0, rows, ROWS, way, i).wait_send()
            gather_copy(1, grads, GRADS, way, i).wait_send()

    done_y = finish(2, part_y, recv_y, got_y, up, LAST)
    end_steps(11, 12, 13)
    for i in range(STEPS):
        for way in WAYS:
            sum_copy(2, part_y, recv_y, way, i).wait_send()
    done_g = finish(3, part_g, recv_g, got_g, down, LAST)
    for i in range(STEPS):
        for way in WAYS:
            sum_copy(3, part_g, recv_g, way, i).wait_send()
    for copy in done_y:
        copy.wait()
    place(weights_y, got_y, out_ref)
    results = [
        pltpu.make_async_copy(out_ref, out_hbm, local_sems.at[7]),
        pltpu.make_async_copy(left_ref, left_hbm, local_sems.at[8]),
    ]
    for copy in results:
        copy.start()
    for copy in done_g + results:
        copy.wait()


def write_out(y_hbm, g_hbm, left_hbm, out_hbm, grad_hbm, y_ref, g_ref, left_ref, dense, in_sems, y_sems, sems):
    tokens, width = y_hbm.shape
    quarter = width // QUARTERS
    needed = [
        pltpu.make_async_copy(g_hbm, g_ref, in_sems.at[0]),
        pltpu.make_async_copy(left_hbm, left_ref, in_sems.at[1]),
    ]
    for copy in needed:
        copy.start()
    part = tokens // QUARTERS
    here = []
    for n in range(QUARTERS):
        rows = pl.ds(n * part, part)
        here.append(pltpu.make_async_copy(y_hbm.at[rows], y_ref.at[rows], in_sems.at[2 + n]))
        here[n].start()
    for copy in needed:
        copy.wait()
    left = left_ref[...]
    copies = []
    for n in range(QUARTERS):
        rows = pl.ds(n * part, part)
        here[n].wait()
        copies.append(pltpu.make_async_copy(y_ref.at[rows], out_hbm.at[rows], y_sems.at[n]))
        copies[n].start()
    cuts = (0, 3, 5, 7)
    for n in range(len(cuts) - 1):
        for i in range(cuts[n], cuts[n + 1]):
            block = g_ref[:, :, i * COLS : (i + 1) * COLS].reshape(STACK, COLS)
            total = dot(left, block).astype(BF16)
            for q in range(QUARTERS):
                dense[:, q * quarter + i * COLS : q * quarter + (i + 1) * COLS] = total[q * tokens : (q + 1) * tokens]
        for q in range(QUARTERS):
            cols = pl.ds(q * quarter + cuts[n] * COLS, (cuts[n + 1] - cuts[n]) * COLS)
            copy = pltpu.make_async_copy(
                dense.at[:, cols], grad_hbm.at[:, cols], sems.at[n * QUARTERS + q]
            )
            copy.start()
            copies.append(copy)
    for copy in copies:
        copy.wait()


def on_device(section_input, cotangent, routes, gate_codes, w_gate, w_up, w_down):
    tokens, width = section_input.shape[1:]
    quarter = width // QUARTERS
    units = w_gate.shape[2]
    count = RING * FLIGHT * CAP
    hbm = pl.BlockSpec(memory_space=pltpu.HBM)
    dma = pltpu.SemaphoreType.DMA
    blocks = pltpu.VMEM((FLIGHT, UNIT, quarter), BF16)
    gathered = pltpu.VMEM((RING, FLIGHT, UNIT, quarter), BF16)
    incoming = pltpu.VMEM((2, 4, FLIGHT, UNIT, quarter), BF16)
    block = pltpu.VMEM((tokens, width), BF16)
    route = pltpu.VMEM(routes.shape[:0:-1], jnp.int32)
    half_wide = pltpu.VMEM((count, 2 * units), F32)
    select = pltpu.VMEM((STACK, tokens), F32)
    dense = jax.ShapeDtypeStruct((tokens, width), BF16)
    out_dense, got_g, left = pl.pallas_call(
        exchange,
        out_shape=(
            dense,
            jax.ShapeDtypeStruct((FLIGHT, UNIT, quarter), BF16),
            jax.ShapeDtypeStruct((QUARTERS * tokens, STACK), BF16),
        ),
        in_specs=[hbm] * 7,
        out_specs=(hbm,) * 3,
        scratch_shapes=[
            block, pltpu.VMEM((QUARTERS * tokens, STACK), BF16), route, route, block, block, blocks, blocks, gathered, gathered,
            pltpu.VMEM((count, width), BF16),
            pltpu.VMEM((width, 4 * units), BF16),
            pltpu.VMEM((2 * units, width), BF16),
            pltpu.VMEM((STACK * QUARTERS, STACK * QUARTERS), BF16),
            pltpu.VMEM((count, 4 * units), F32),
            half_wide,
            half_wide,
            pltpu.VMEM((count, 2 * units), BF16),
            half_wide,
            pltpu.VMEM((count, 4 * units), BF16),
            gathered, gathered, incoming, incoming, blocks,
            select, select, select, select,
            dma((9,)),
            dma((3,)), dma((3,)),
            dma((2, FLIGHT)), dma((2, FLIGHT)),
            dma((2,)), dma((2,)),
            dma((4, 2, MOST)), dma((4, 2, MOST)),
            dma((2, FLIGHT)), dma((2, FLIGHT)),
        ],
        compiler_params=pltpu.CompilerParams(
            collective_id=0, has_side_effects=True, vmem_limit_bytes=57 * 2**20
        ),
        cost_estimate=pl.CostEstimate(
            flops=24 * count * width * units, bytes_accessed=14 * tokens * width, transcendentals=0
        ),
        name="exchange",
    )(routes[0].T, gate_codes[0].T, section_input[0], cotangent[0], w_gate[0], w_up[0], w_down[0])
    passed, grad_passed = pl.pallas_call(
        write_out,
        out_shape=(dense,) * 2,
        in_specs=[hbm] * 3,
        out_specs=(hbm,) * 2,
        scratch_shapes=[
            block, blocks, pltpu.VMEM((QUARTERS * tokens, STACK), BF16), block,
            dma((2 + QUARTERS,)), dma((QUARTERS,)), dma((3 * QUARTERS,)),
        ],
        compiler_params=pltpu.CompilerParams(vmem_limit_bytes=57 * 2**20),
        name="write_out",
    )(out_dense, got_g, left)
    return passed[None], grad_passed[None]


def solution(mesh):
    placed = (
        P("pipe", "expert", None),
        P("pipe", "expert", None),
        P("pipe", "expert", None),
        P("pipe", "expert", None),
        P("pipe", None, "expert"),
        P("pipe", None, "expert"),
        P("pipe", "expert", None),
    )
    return jax.shard_map(
        on_device,
        mesh=mesh,
        in_specs=placed,
        out_specs=(P("pipe", "expert", None), P("pipe", "expert", None)),
        check_vma=False,
    )
```

```python
import jax
import jax.numpy as jnp
from jax import lax
from jax.experimental import pallas as pl
from jax.experimental.pallas import tpu as pltpu
from jax.sharding import PartitionSpec as P

CAP = 4
TOP = 8
FLIGHT = 4
QUARTERS = 4
CORES = 2
RING = 8
UNIT = QUARTERS * CAP
STACK = FLIGHT * UNIT
COLS = 256
TILE = 512
MESH = pl.DeviceIdType.MESH
F32 = jnp.float32
BF16 = jnp.bfloat16

RIGHT, LEFT = 0, 1
WAYS = (RIGHT, LEFT)
FROM = {RIGHT: (0, 1, 3, 5, 7), LEFT: (0, 2, 4, 6, 7)}
ROWS = {
    RIGHT: tuple((hops, j, 1) for hops, order in ((0, (0, 1, 3, 2)), (1, (0, 1, 3, 2)), (2, (0, 1, 3, 2)), (3, (0, 1))) for j in order),
    LEFT: tuple((hops, j, 1) for hops, order in ((0, (0, 3, 1, 2)), (1, (3, 0, 2, 1)), (2, (3, 2, 0, 1)), (3, (3, 2))) for j in order),
}
GRADS = {
    RIGHT: ROWS[RIGHT],
    LEFT: tuple((hops, j, 1) for hops, order in ((0, (0, 3, 2, 1)), (1, (3, 2, 0, 1)), (2, (3, 2, 0, 1)), (3, (3, 2))) for j in order),
}
LAST = (1, 2, 3, 0)
ENDS = {
    LEFT: tuple((hops, j, 1) for hops, order in ((4, (1, 3)), (3, (2, 0, 1, 3)), (2, (2, 1, 0, 3)), (1, LAST)) for j in order),
    RIGHT: tuple((hops, j, 1) for hops, order in ((4, (2, 0)), (3, (1, 3, 2, 0)), (2, (1, 3, 2, 0)), (1, LAST)) for j in order),
}
OUTS = {
    LEFT: tuple((hops, j, 1) for hops, order in ((4, (1, 3)), (3, (2, 0, 1, 3)), (2, (2, 0, 1, 3)), (1, (2, 0, 1, 3))) for j in order),
    RIGHT: tuple((hops, j, 1) for hops, order in ((4, (2, 0)), (3, (1, 3, 2, 0)), (2, (1, 3, 2, 0)), (1, (1, 3, 2, 0))) for j in order),
}
STEPS = len(ENDS[LEFT])
ORDERS = (ROWS, GRADS, OUTS, ENDS)
MOST = max(len(order[way]) for order in ORDERS for way in WAYS)


def nt(left, right):
    return lax.dot_general(left, right, (((1,), (1,)), ((), ())), preferred_element_type=F32)


def tn(left, right):
    return lax.dot_general(left, right, (((0,), (0,)), ((), ())), preferred_element_type=F32)


def dot(left, right):
    return jnp.dot(left, right, preferred_element_type=F32)


def iota(shape, dim):
    return lax.broadcasted_iota(jnp.int32, shape, dim)


def exchange(
    routing_ref, tok_hbm, cot_hbm, wg_ref, wu_ref, wd_ref,
    out_ref, got_g, left_ref,
    tok, cot, pick_x, pick_g, rows, grads, nat, gu, wd, swap, acc, a_gate, a_up, hid, dh, dgu,
    part_y, part_g, recv_y, recv_g, got_y, sel, wsel, sel_in, wsel_in,
    local_sems, w_send, w_recv, x_send, x_recv, s_send, s_recv,
    ring_send, ring_recv, fin_send, fin_recv,
):
    me = lax.axis_index("expert")
    y = lax.axis_index("pipe")
    pipes = lax.axis_size("pipe")
    core = lax.rem(me, CORES)
    z = lax.rem(lax.div(me, CORES), RING)
    x = lax.div(me, CORES * RING)
    tokens, width = tok.shape
    quarter = width // QUARTERS
    units = wg_ref.shape[1]
    count = nat.shape[0]

    def at(xx, zz, cc, yy):
        return ((xx * RING + zz) * CORES + cc, yy)

    ahead = lax.rem(y + 1, pipes)
    behind = lax.rem(y + pipes - 1, pipes)
    sibling = at(x, z, 1 - core, y)
    next_on = {
        RIGHT: at(x, lax.rem(z + 1, RING), core, y),
        LEFT: at(x, lax.rem(z + RING - 1, RING), core, y),
    }
    plane = [lax.rem(x + k, FLIGHT) for k in range(FLIGHT)]
    across = [at(xx, z, core, y) for xx in plane]
    up = [at(xx, z, core, ahead) for xx in plane]
    down = [at(xx, z, core, behind) for xx in plane]

    own = [
        pltpu.make_async_copy(tok_hbm, tok, local_sems.at[0]),
        pltpu.make_async_copy(cot_hbm, cot, local_sems.at[1]),
        pltpu.make_async_copy(wg_ref, gu.at[:, pl.ds(0, units)], local_sems.at[2]),
        pltpu.make_async_copy(wu_ref, gu.at[:, pl.ds(2 * units, units)], local_sems.at[3]),
        pltpu.make_async_copy(wd_ref, wd.at[pl.ds(0, units)], local_sems.at[4]),
    ]
    own[0].start()

    barrier = pltpu.get_barrier_semaphore()
    peers = [sibling, next_on[RIGHT], next_on[LEFT]] + across[1:] + up + down
    for peer in peers:
        pl.semaphore_signal(barrier, inc=1, device_id=peer, device_id_type=MESH)

    def remote(src, dst, send, recv, device):
        return pltpu.make_async_remote_copy(
            src_ref=src, dst_ref=dst, send_sem=send, recv_sem=recv,
            device_id=device, device_id_type=MESH,
        )

    routes = routing_ref[:TOP]
    codes = routing_ref[TOP:].astype(F32)
    ratio = 2.5 * codes / jnp.sum(codes, axis=0, keepdims=True)
    named = [routes == f for f in range(FLIGHT)]
    matched = [jnp.sum(jnp.where(hit, 1.0, 0.0), axis=0, keepdims=True) for hit in named]
    weight = [jnp.sum(jnp.where(hit, ratio, 0.0), axis=0, keepdims=True) for hit in named]
    eight = (2 * FLIGHT, tokens)
    stacked = jnp.zeros(eight, F32)
    for f in range(FLIGHT):
        stacked = jnp.where(iota(eight, 0) == f, matched[f], stacked)
    upto = (iota((tokens, tokens), 0) <= iota((tokens, tokens), 1)).astype(F32).astype(BF16)
    rank = dot(stacked.astype(BF16), upto)
    slot = ((iota((UNIT, tokens), 0) & (CAP - 1)) + 1).astype(F32)
    for f in range(FLIGHT):
        here = jnp.where((matched[f] == 1.0) & (rank[f : f + 1] == slot), 1.0, 0.0)
        sel[pl.ds(UNIT * f, UNIT)] = here
        wsel[pl.ds(UNIT * f, UNIT)] = here * weight[f]

    def choose(block, out, scale, first, last):
        quarter_of = (iota((STACK, tokens), 0) // CAP) & (QUARTERS - 1)
        picks = [jnp.where(quarter_of == q, sel[...], 0.0).astype(BF16) for q in range(QUARTERS)]
        for i in range(first, last):
            total = sum(
                dot(picks[q], block[:, q * quarter + i * COLS : q * quarter + (i + 1) * COLS])
                for q in range(QUARTERS)
            )
            if scale is not None:
                total = total * scale
            out[:, :, i * COLS : (i + 1) * COLS] = total.astype(BF16).reshape(FLIGHT, UNIT, COLS)

    def x_copy(i, src, buf, k):
        return remote(
            src.at[plane[k]], buf.at[0, FLIGHT - k], x_send.at[i, k], x_recv.at[i, k], across[k]
        )

    def part_of(buf, place, first, n):
        return buf.at[place, pl.ds(first, n)]

    def gather_copy(kind, buf, order, way, i):
        hops, first, n = order[way][i]
        return remote(
            part_of(buf, FROM[way][hops], first, n), part_of(buf, FROM[way][hops + 1], first, n),
            ring_send.at[kind, way, i], ring_recv.at[kind, way, i], next_on[way],
        )

    arrived = set()

    def arrive(kind, src, buf, order, way, hops, first, n):
        if hops == 0:
            for j in range(max(first, 1), first + n):
                if (kind, j) not in arrived:
                    arrived.add((kind, j))
                    x_copy(kind, src, buf, FLIGHT - j).wait_recv()
            return
        for i, (h, f, m) in enumerate(order[way]):
            if h == hops - 1 and f < first + n and first < f + m and (kind, way, i) not in arrived:
                arrived.add((kind, way, i))
                gather_copy(kind, buf, order, way, i).wait_recv()

    def gather_step(kind, src, buf, order, i):
        for way in WAYS:
            arrive(kind, src, buf, order, way, *order[way][i])
            gather_copy(kind, buf, order, way, i).start()

    def gather_end(kind, src, buf, order):
        for hops in (3, 4):
            for way in WAYS:
                arrive(kind, src, buf, order, way, hops, 0, FLIGHT)

    def sum_copy(kind, part, recv, way, i):
        hops, first, n = ORDERS[kind][way][i]
        return remote(
            part_of(part, FROM[1 - way][hops], first, n), recv.at[way, hops - 1, pl.ds(first, n)],
            ring_send.at[kind, way, i], ring_recv.at[kind, way, i], next_on[way],
        )

    def sum_arrive(kind, part, recv, way, hops, first, n):
        came = False
        for i, (h, f, m) in enumerate(ORDERS[kind][way]):
            if h == hops + 1 and f < first + n and first < f + m:
                came = True
                if (kind, way, i) not in arrived:
                    arrived.add((kind, way, i))
                    sum_copy(kind, part, recv, way, i).wait_recv()
        return came

    def sum_step(kind, part, recv, i):
        for way in WAYS:
            hops, first, n = ORDERS[kind][way][i]
            if sum_arrive(kind, part, recv, way, hops, first, n):
                here, there = (FROM[1 - way][hops], pl.ds(first, n)), (way, hops, pl.ds(first, n))
                part[here] = (part[here].astype(F32) + recv[there].astype(F32)).astype(BF16)
            sum_copy(kind, part, recv, way, i).start()

    def finish(kind, part, recv, got, targets, order):
        copies = []
        for j in order:
            for way in WAYS:
                sum_arrive(kind, part, recv, way, 0, j, 1)
            total = part[0, j].astype(F32) + recv[LEFT, 0, j].astype(F32)
            part[0, j] = (total + recv[RIGHT, 0, j].astype(F32)).astype(BF16)
            copy = remote(
                part.at[0, j], got.at[x], fin_send.at[kind - 2, j], fin_recv.at[kind - 2, j], targets[j]
            )
            copy.start()
            copies.append(copy)
        return copies

    def regrouping(dim):
        size = (STACK * QUARTERS, STACK * QUARTERS)
        n, m = iota(size, dim), iota(size, 1 - dim)
        low = n & (STACK - 1)
        there = (low // CAP) * UNIT + (n // STACK) * CAP + (low & (CAP - 1))
        return (m == there).astype(F32).astype(BF16)

    def cols_of(i, q=0):
        start = q * quarter + i * COLS
        return pl.ds(start if isinstance(start, int) else pl.multiple_of(start, COLS), COLS)

    def natural(buf, group):
        for i in range(quarter // COLS):
            block = buf[pl.ds(4 * group, 4), :, :, cols_of(i)].reshape(STACK * QUARTERS, COLS)
            got = dot(swap[...], block).astype(BF16)
            for q in range(QUARTERS):
                nat[pl.ds(STACK * group, STACK), cols_of(i, q)] = got[q * STACK : (q + 1) * STACK]

    def blocked(product, part, first, last):
        for i in range(first, last):
            pieces = [product(cols_of(i, q)).astype(BF16) for q in range(QUARTERS)]
            for group in range(count // STACK):
                block = jnp.concatenate([p[STACK * group : STACK * (group + 1)] for p in pieces], axis=0)
                got = tn(swap[...], block).astype(BF16)
                part[pl.ds(4 * group, 4), :, :, cols_of(i)] = got.reshape(4, FLIGHT, UNIT, COLS)

    def gate_up(first, last):
        ks = pl.ds(first * TILE, (last - first) * TILE)
        for n in range(0, 4 * units, COLS):
            cols = pl.ds(n, COLS)
            acc[:, cols] += dot(nat[:, ks], gu[ks, cols])

    def activate():
        gate, upper = acc[:, : 2 * units], acc[:, 2 * units :]
        sigma = jax.nn.sigmoid(gate)
        silu = gate * sigma
        hid[...] = (silu * upper).astype(BF16)
        a_gate[...] = upper * sigma * (1.0 + gate * (1.0 - sigma))
        a_up[...] = silu

    def outputs(first, last):
        blocked(lambda cols: dot(hid[...], wd[:, cols]), part_y, first, last)

    def d_hidden(first, last):
        ks = pl.ds(first * TILE, (last - first) * TILE)
        dh[...] += nt(nat[:, ks], wd[:, ks])

    def d_activate():
        dgu[:, : 2 * units] = (dh[...] * a_gate[...]).astype(BF16)
        dgu[:, 2 * units :] = (dh[...] * a_up[...]).astype(BF16)

    def d_inputs(first, last):
        blocked(lambda cols: nt(dgu[...], gu[cols, :]), part_g, first, last)

    def by_quarter(weights):
        quarter_of = (iota(weights.shape, 1) // CAP) & (QUARTERS - 1)
        return jnp.concatenate(
            [jnp.where(quarter_of == q, weights, 0.0).astype(BF16) for q in range(QUARTERS)], axis=0
        )

    def place(left, got, out):
        terms = left.shape[1] // STACK
        for i in range(quarter // COLS):
            block = got[:, :, cols_of(i)].reshape(STACK, COLS)
            total = dot(left, jnp.concatenate([block] * terms, axis=0)).astype(BF16)
            for q in range(QUARTERS):
                out[:, cols_of(i, q)] = total[q * tokens : (q + 1) * tokens]

    def three_terms(weights):
        high = weights.astype(BF16).astype(F32)
        mid = (weights - high).astype(BF16).astype(F32)
        low = (weights - high - mid).astype(BF16).astype(F32)
        ends = jnp.concatenate([low, jnp.zeros_like(low)], axis=0).T
        return jnp.concatenate([jnp.concatenate([high, mid], axis=0).T, ends[:, :STACK]], axis=1)

    tiles = width // TILE
    steps = quarter // COLS

    own[0].wait()
    own[1].start()
    choose(tok, pick_x, None, 0, steps)
    pl.semaphore_wait(barrier, len(peers))
    x_copies = [x_copy(0, pick_x, rows, k) for k in (1, 3, 2)]
    for copy in x_copies:
        copy.start()
    rows[0, 0] = pick_x[x]
    def row_steps(*which):
        for i in which:
            gather_step(0, pick_x, rows, ROWS, i)

    def grad_steps(*which):
        for i in which:
            gather_step(1, pick_g, grads, GRADS, i)

    def out_steps(*which):
        for i in which:
            sum_step(2, part_y, recv_y, i)

    def end_steps(*which):
        for i in which:
            sum_step(3, part_g, recv_g, i)

    row_steps(0)
    own[1].wait()
    for copy in own[2:]:
        copy.start()
    choose(cot, pick_g, jnp.sum(wsel[...], axis=1, keepdims=True), 0, steps)
    g_copies = [x_copy(1, pick_g, grads, k) for k in (1, 3, 2)]
    for copy in g_copies:
        copy.start()
    grads[0, 0] = pick_g[x]
    grad_steps(0)
    row_steps(1, 2)
    grad_steps(1, 2)
    row_steps(3, 4)
    small = [
        remote(wsel, wsel_in, s_send.at[0], s_recv.at[0], up[0]),
        remote(sel, sel_in, s_send.at[1], s_recv.at[1], down[0]),
    ]
    other = [
        remote(wg_ref, gu.at[:, pl.ds(units, units)], w_send.at[0], w_recv.at[0], sibling),
        remote(wu_ref, gu.at[:, pl.ds(3 * units, units)], w_send.at[1], w_recv.at[1], sibling),
        remote(wd_ref, wd.at[pl.ds(units, units)], w_send.at[2], w_recv.at[2], sibling),
    ]
    for copy in other + small:
        copy.start()
    row_steps(5, 6)
    swap[...] = regrouping(0)
    row_steps(7, 8)
    acc[...] = jnp.zeros_like(acc)
    dh[...] = jnp.zeros_like(dh)
    row_steps(9, 10, 11, 12, 13)
    grad_steps(3, 4)
    arrive(0, pick_x, rows, ROWS, RIGHT, 2, 0, FLIGHT)
    natural(rows, 0)
    grad_steps(5)

    gather_end(0, pick_x, rows, ROWS)
    natural(rows, 1)
    for copy in own[2:]:
        copy.wait()
    for copy in other:
        copy.wait_recv()
    grad_steps(6)
    gate_up(0, tiles // 2)
    grad_steps(7, 8)
    gate_up(tiles // 2, tiles)
    activate()
    grad_steps(9, 10)
    outputs(0, 2)
    grad_steps(11)
    outputs(2, 4)
    grad_steps(12)
    outputs(4, 6)
    grad_steps(13)
    outputs(6, steps)

    out_steps(0, 1)
    arrive(1, pick_g, grads, GRADS, RIGHT, 2, 0, FLIGHT)
    natural(grads, 0)
    out_steps(2)
    gather_end(1, pick_g, grads, GRADS)
    natural(grads, 1)
    out_steps(3)
    d_hidden(0, tiles)
    d_activate()
    out_steps(4, 5)
    d_inputs(0, 2)
    out_steps(6, 7)
    d_inputs(2, 4)
    out_steps(8)
    d_inputs(4, 6)
    out_steps(9)
    d_inputs(6, steps)
    end_steps(0, 1)
    out_steps(10)
    end_steps(2, 3)
    small[0].wait_recv()
    weights_y = by_quarter(three_terms(wsel_in[...]))
    small[1].wait_recv()
    left_ref[...] = by_quarter(jnp.concatenate([sel_in[...], jnp.zeros_like(sel_in)], axis=0).T[:, :STACK])
    out_steps(11)
    end_steps(4, 5)
    for copy in x_copies + g_copies + other + small:
        copy.wait_send()
    out_steps(12)
    end_steps(6, 7)
    out_steps(13)
    end_steps(8, 9, 10)
    for i in range(STEPS):
        for way in WAYS:
            gather_copy(0, rows, ROWS, way, i).wait_send()
            gather_copy(1, grads, GRADS, way, i).wait_send()

    done_y = finish(2, part_y, recv_y, got_y, up, LAST)
    end_steps(11, 12, 13)
    for i in range(STEPS):
        for way in WAYS:
            sum_copy(2, part_y, recv_y, way, i).wait_send()
    done_g = finish(3, part_g, recv_g, got_g, down, LAST)
    for i in range(STEPS):
        for way in WAYS:
            sum_copy(3, part_g, recv_g, way, i).wait_send()
    for copy in done_y:
        copy.wait()
    place(weights_y, got_y, out_ref)
    for copy in done_g:
        copy.wait()


def write_out(y_ref, g_ref, left_ref, out_hbm, grad_hbm, dense, sems):
    tokens, width = y_ref.shape
    quarter = width // QUARTERS
    copies = [pltpu.make_async_copy(y_ref, out_hbm, sems.at[3 * QUARTERS])]
    copies[0].start()
    left = left_ref[...]
    cuts = (0, 3, 5, 7)
    for n in range(len(cuts) - 1):
        for i in range(cuts[n], cuts[n + 1]):
            block = g_ref[:, :, i * COLS : (i + 1) * COLS].reshape(STACK, COLS)
            total = dot(left, block).astype(BF16)
            for q in range(QUARTERS):
                dense[:, q * quarter + i * COLS : q * quarter + (i + 1) * COLS] = total[q * tokens : (q + 1) * tokens]
        for q in range(QUARTERS):
            cols = pl.ds(q * quarter + cuts[n] * COLS, (cuts[n + 1] - cuts[n]) * COLS)
            copy = pltpu.make_async_copy(
                dense.at[:, cols], grad_hbm.at[:, cols], sems.at[n * QUARTERS + q]
            )
            copy.start()
            copies.append(copy)
    for copy in copies:
        copy.wait()


def on_device(section_input, cotangent, routes, gate_codes, w_gate, w_up, w_down):
    tokens, width = section_input.shape[1:]
    quarter = width // QUARTERS
    units = w_gate.shape[2]
    count = RING * FLIGHT * CAP
    vmem = pl.BlockSpec(memory_space=pltpu.VMEM)
    hbm = pl.BlockSpec(memory_space=pltpu.HBM)
    dma = pltpu.SemaphoreType.DMA
    blocks = pltpu.VMEM((FLIGHT, UNIT, quarter), BF16)
    gathered = pltpu.VMEM((RING, FLIGHT, UNIT, quarter), BF16)
    incoming = pltpu.VMEM((2, 4, FLIGHT, UNIT, quarter), BF16)
    block = pltpu.VMEM((tokens, width), BF16)
    half_wide = pltpu.VMEM((count, 2 * units), F32)
    select = pltpu.VMEM((STACK, tokens), F32)
    dense = jax.ShapeDtypeStruct((tokens, width), BF16)
    out_dense, got_g, left = pl.pallas_call(
        exchange,
        out_shape=(
            dense,
            jax.ShapeDtypeStruct((FLIGHT, UNIT, quarter), BF16),
            jax.ShapeDtypeStruct((QUARTERS * tokens, STACK), BF16),
        ),
        in_specs=[vmem] + [hbm] * 5,
        out_specs=(vmem,) * 3,
        scratch_shapes=[
            block, block, blocks, blocks, gathered, gathered,
            pltpu.VMEM((count, width), BF16),
            pltpu.VMEM((width, 4 * units), BF16),
            pltpu.VMEM((2 * units, width), BF16),
            pltpu.VMEM((STACK * QUARTERS, STACK * QUARTERS), BF16),
            pltpu.VMEM((count, 4 * units), F32),
            half_wide,
            half_wide,
            pltpu.VMEM((count, 2 * units), BF16),
            half_wide,
            pltpu.VMEM((count, 4 * units), BF16),
            gathered, gathered, incoming, incoming, blocks,
            select, select, select, select,
            dma((5,)),
            dma((3,)), dma((3,)),
            dma((2, FLIGHT)), dma((2, FLIGHT)),
            dma((2,)), dma((2,)),
            dma((4, 2, MOST)), dma((4, 2, MOST)),
            dma((2, FLIGHT)), dma((2, FLIGHT)),
        ],
        compiler_params=pltpu.CompilerParams(
            collective_id=0, has_side_effects=True, vmem_limit_bytes=51 * 2**20
        ),
        cost_estimate=pl.CostEstimate(
            flops=24 * count * width * units, bytes_accessed=14 * tokens * width, transcendentals=0
        ),
        name="exchange",
    )(jnp.concatenate([routes[0].T, gate_codes[0].T]), section_input[0], cotangent[0], w_gate[0], w_up[0], w_down[0])
    passed, grad_passed = pl.pallas_call(
        write_out,
        out_shape=(dense,) * 2,
        in_specs=[vmem] * 3,
        out_specs=(hbm,) * 2,
        scratch_shapes=[block, dma((1 + 3 * QUARTERS,))],
        compiler_params=pltpu.CompilerParams(vmem_limit_bytes=51 * 2**20),
        name="write_out",
    )(out_dense, got_g, left)
    return passed[None], grad_passed[None]


def solution(mesh):
    placed = (
        P("pipe", "expert", None),
        P("pipe", "expert", None),
        P("pipe", "expert", None),
        P("pipe", "expert", None),
        P("pipe", None, "expert"),
        P("pipe", None, "expert"),
        P("pipe", "expert", None),
    )
    return jax.shard_map(
        on_device,
        mesh=mesh,
        in_specs=placed,
        out_specs=(P("pipe", "expert", None), P("pipe", "expert", None)),
        check_vma=False,
    )
```

```python
import jax
import jax.numpy as jnp
from jax import lax
from jax.experimental import pallas as pl
from jax.experimental.pallas import tpu as pltpu
from jax.sharding import PartitionSpec as P

CAP = 4
TOP = 8
FLIGHT = 4
QUARTERS = 4
CORES = 2
RING = 8
UNIT = QUARTERS * CAP
STACK = FLIGHT * UNIT
COLS = 256
TILE = 512
MESH = pl.DeviceIdType.MESH
F32 = jnp.float32
BF16 = jnp.bfloat16

RIGHT, LEFT = 0, 1
WAYS = (RIGHT, LEFT)
FROM = {RIGHT: (0, 1, 3, 5, 7), LEFT: (0, 2, 4, 6, 7)}
ROWS = {
    RIGHT: tuple((hops, j, 1) for hops, order in ((0, (0, 1, 3, 2)), (1, (0, 1, 3, 2)), (2, (0, 1, 3, 2)), (3, (0, 1))) for j in order),
    LEFT: tuple((hops, j, 1) for hops, order in ((0, (0, 3, 1, 2)), (1, (3, 0, 2, 1)), (2, (3, 2, 0, 1)), (3, (3, 2))) for j in order),
}
GRADS = {
    RIGHT: ROWS[RIGHT],
    LEFT: tuple((hops, j, 1) for hops, order in ((0, (0, 3, 2, 1)), (1, (3, 2, 0, 1)), (2, (3, 2, 0, 1)), (3, (3, 2))) for j in order),
}
LAST = (1, 2, 3, 0)
ENDS = {
    LEFT: tuple((hops, j, 1) for hops, order in ((4, (1, 3)), (3, (2, 0, 1, 3)), (2, (2, 1, 0, 3)), (1, LAST)) for j in order),
    RIGHT: tuple((hops, j, 1) for hops, order in ((4, (2, 0)), (3, (1, 3, 2, 0)), (2, (1, 3, 2, 0)), (1, LAST)) for j in order),
}
OUTS = {
    LEFT: tuple((hops, j, 1) for hops, order in ((4, (1, 3)), (3, (2, 0, 1, 3)), (2, (2, 0, 1, 3)), (1, (2, 0, 1, 3))) for j in order),
    RIGHT: tuple((hops, j, 1) for hops, order in ((4, (2, 0)), (3, (1, 3, 2, 0)), (2, (1, 3, 2, 0)), (1, (1, 3, 2, 0))) for j in order),
}
STEPS = len(ENDS[LEFT])
ORDERS = (ROWS, GRADS, OUTS, ENDS)
MOST = max(len(order[way]) for order in ORDERS for way in WAYS)


def nt(left, right):
    return lax.dot_general(left, right, (((1,), (1,)), ((), ())), preferred_element_type=F32)


def tn(left, right):
    return lax.dot_general(left, right, (((0,), (0,)), ((), ())), preferred_element_type=F32)


def dot(left, right):
    return jnp.dot(left, right, preferred_element_type=F32)


def iota(shape, dim):
    return lax.broadcasted_iota(jnp.int32, shape, dim)


def exchange(
    routing_ref, tok_hbm, cot_hbm, wg_ref, wu_ref, wd_ref,
    out_ref, got_g, left_ref,
    tok, cot, pick_x, pick_g, rows, grads, nat, gu, wd, swap, acc, a_gate, a_up, hid, dh, dgu,
    part_y, part_g, recv_y, recv_g, got_y, sel, wsel, sel_in, wsel_in,
    local_sems, w_send, w_recv, x_send, x_recv, s_send, s_recv,
    ring_send, ring_recv, fin_send, fin_recv,
):
    me = lax.axis_index("expert")
    y = lax.axis_index("pipe")
    pipes = lax.axis_size("pipe")
    core = lax.rem(me, CORES)
    z = lax.rem(lax.div(me, CORES), RING)
    x = lax.div(me, CORES * RING)
    tokens, width = tok.shape
    quarter = width // QUARTERS
    units = wg_ref.shape[1]
    count = nat.shape[0]

    def at(xx, zz, cc, yy):
        return ((xx * RING + zz) * CORES + cc, yy)

    ahead = lax.rem(y + 1, pipes)
    behind = lax.rem(y + pipes - 1, pipes)
    sibling = at(x, z, 1 - core, y)
    next_on = {
        RIGHT: at(x, lax.rem(z + 1, RING), core, y),
        LEFT: at(x, lax.rem(z + RING - 1, RING), core, y),
    }
    plane = [lax.rem(x + k, FLIGHT) for k in range(FLIGHT)]
    across = [at(xx, z, core, y) for xx in plane]
    up = [at(xx, z, core, ahead) for xx in plane]
    down = [at(xx, z, core, behind) for xx in plane]

    own = [
        pltpu.make_async_copy(tok_hbm, tok, local_sems.at[0]),
        pltpu.make_async_copy(cot_hbm, cot, local_sems.at[1]),
        pltpu.make_async_copy(wg_ref, gu.at[:, pl.ds(0, units)], local_sems.at[2]),
        pltpu.make_async_copy(wu_ref, gu.at[:, pl.ds(2 * units, units)], local_sems.at[3]),
        pltpu.make_async_copy(wd_ref, wd.at[pl.ds(0, units)], local_sems.at[4]),
    ]
    own[0].start()

    barrier = pltpu.get_barrier_semaphore()
    peers = [sibling, next_on[RIGHT], next_on[LEFT]] + across[1:] + up + down
    for peer in peers:
        pl.semaphore_signal(barrier, inc=1, device_id=peer, device_id_type=MESH)

    def remote(src, dst, send, recv, device):
        return pltpu.make_async_remote_copy(
            src_ref=src, dst_ref=dst, send_sem=send, recv_sem=recv,
            device_id=device, device_id_type=MESH,
        )

    routes = routing_ref[:TOP]
    codes = routing_ref[TOP:].astype(F32)
    ratio = 2.5 * codes / jnp.sum(codes, axis=0, keepdims=True)
    named = [routes == f for f in range(FLIGHT)]
    matched = [jnp.sum(jnp.where(hit, 1.0, 0.0), axis=0, keepdims=True) for hit in named]
    weight = [jnp.sum(jnp.where(hit, ratio, 0.0), axis=0, keepdims=True) for hit in named]
    eight = (2 * FLIGHT, tokens)
    stacked = jnp.zeros(eight, F32)
    for f in range(FLIGHT):
        stacked = jnp.where(iota(eight, 0) == f, matched[f], stacked)
    upto = (iota((tokens, tokens), 0) <= iota((tokens, tokens), 1)).astype(F32).astype(BF16)
    rank = dot(stacked.astype(BF16), upto)
    slot = ((iota((UNIT, tokens), 0) & (CAP - 1)) + 1).astype(F32)
    for f in range(FLIGHT):
        here = jnp.where((matched[f] == 1.0) & (rank[f : f + 1] == slot), 1.0, 0.0)
        sel[pl.ds(UNIT * f, UNIT)] = here
        wsel[pl.ds(UNIT * f, UNIT)] = here * weight[f]

    def choose(block, out, scale, first, last):
        quarter_of = (iota((STACK, tokens), 0) // CAP) & (QUARTERS - 1)
        picks = [jnp.where(quarter_of == q, sel[...], 0.0).astype(BF16) for q in range(QUARTERS)]
        for i in range(first, last):
            total = sum(
                dot(picks[q], block[:, q * quarter + i * COLS : q * quarter + (i + 1) * COLS])
                for q in range(QUARTERS)
            )
            if scale is not None:
                total = total * scale
            out[:, :, i * COLS : (i + 1) * COLS] = total.astype(BF16).reshape(FLIGHT, UNIT, COLS)

    def x_copy(i, src, buf, k):
        return remote(
            src.at[plane[k]], buf.at[0, FLIGHT - k], x_send.at[i, k], x_recv.at[i, k], across[k]
        )

    def part_of(buf, place, first, n):
        return buf.at[place, pl.ds(first, n)]

    def gather_copy(kind, buf, order, way, i):
        hops, first, n = order[way][i]
        return remote(
            part_of(buf, FROM[way][hops], first, n), part_of(buf, FROM[way][hops + 1], first, n),
            ring_send.at[kind, way, i], ring_recv.at[kind, way, i], next_on[way],
        )

    arrived = set()

    def arrive(kind, src, buf, order, way, hops, first, n):
        if hops == 0:
            for j in range(max(first, 1), first + n):
                if (kind, j) not in arrived:
                    arrived.add((kind, j))
                    x_copy(kind, src, buf, FLIGHT - j).wait_recv()
            return
        for i, (h, f, m) in enumerate(order[way]):
            if h == hops - 1 and f < first + n and first < f + m and (kind, way, i) not in arrived:
                arrived.add((kind, way, i))
                gather_copy(kind, buf, order, way, i).wait_recv()

    def gather_step(kind, src, buf, order, i):
        for way in WAYS:
            arrive(kind, src, buf, order, way, *order[way][i])
            gather_copy(kind, buf, order, way, i).start()

    def gather_end(kind, src, buf, order):
        for hops in (3, 4):
            for way in WAYS:
                arrive(kind, src, buf, order, way, hops, 0, FLIGHT)

    def sum_copy(kind, part, recv, way, i):
        hops, first, n = ORDERS[kind][way][i]
        return remote(
            part_of(part, FROM[1 - way][hops], first, n), recv.at[way, hops - 1, pl.ds(first, n)],
            ring_send.at[kind, way, i], ring_recv.at[kind, way, i], next_on[way],
        )

    def sum_arrive(kind, part, recv, way, hops, first, n):
        came = False
        for i, (h, f, m) in enumerate(ORDERS[kind][way]):
            if h == hops + 1 and f < first + n and first < f + m:
                came = True
                if (kind, way, i) not in arrived:
                    arrived.add((kind, way, i))
                    sum_copy(kind, part, recv, way, i).wait_recv()
        return came

    def sum_step(kind, part, recv, i):
        for way in WAYS:
            hops, first, n = ORDERS[kind][way][i]
            if sum_arrive(kind, part, recv, way, hops, first, n):
                here, there = (FROM[1 - way][hops], pl.ds(first, n)), (way, hops, pl.ds(first, n))
                part[here] = (part[here].astype(F32) + recv[there].astype(F32)).astype(BF16)
            sum_copy(kind, part, recv, way, i).start()

    def finish(kind, part, recv, got, targets, order):
        copies = []
        for j in order:
            for way in WAYS:
                sum_arrive(kind, part, recv, way, 0, j, 1)
            total = part[0, j].astype(F32) + recv[LEFT, 0, j].astype(F32)
            part[0, j] = (total + recv[RIGHT, 0, j].astype(F32)).astype(BF16)
            copy = remote(
                part.at[0, j], got.at[x], fin_send.at[kind - 2, j], fin_recv.at[kind - 2, j], targets[j]
            )
            copy.start()
            copies.append(copy)
        return copies

    def regrouping(dim):
        size = (STACK * QUARTERS, STACK * QUARTERS)
        n, m = iota(size, dim), iota(size, 1 - dim)
        low = n & (STACK - 1)
        there = (low // CAP) * UNIT + (n // STACK) * CAP + (low & (CAP - 1))
        return (m == there).astype(F32).astype(BF16)

    def cols_of(i, q=0):
        start = q * quarter + i * COLS
        return pl.ds(start if isinstance(start, int) else pl.multiple_of(start, COLS), COLS)

    def natural(buf, group):
        for i in range(quarter // COLS):
            block = buf[pl.ds(4 * group, 4), :, :, cols_of(i)].reshape(STACK * QUARTERS, COLS)
            got = dot(swap[...], block).astype(BF16)
            for q in range(QUARTERS):
                nat[pl.ds(STACK * group, STACK), cols_of(i, q)] = got[q * STACK : (q + 1) * STACK]

    def blocked(product, part, first, last):
        for i in range(first, last):
            pieces = [product(cols_of(i, q)).astype(BF16) for q in range(QUARTERS)]
            for group in range(count // STACK):
                block = jnp.concatenate([p[STACK * group : STACK * (group + 1)] for p in pieces], axis=0)
                got = tn(swap[...], block).astype(BF16)
                part[pl.ds(4 * group, 4), :, :, cols_of(i)] = got.reshape(4, FLIGHT, UNIT, COLS)

    def gate_up(first, last):
        ks = pl.ds(first * TILE, (last - first) * TILE)
        for n in range(0, 4 * units, COLS):
            cols = pl.ds(n, COLS)
            acc[:, cols] += dot(nat[:, ks], gu[ks, cols])

    def activate():
        gate, upper = acc[:, : 2 * units], acc[:, 2 * units :]
        sigma = jax.nn.sigmoid(gate)
        silu = gate * sigma
        hid[...] = (silu * upper).astype(BF16)
        a_gate[...] = upper * sigma * (1.0 + gate * (1.0 - sigma))
        a_up[...] = silu

    def outputs(first, last):
        blocked(lambda cols: dot(hid[...], wd[:, cols]), part_y, first, last)

    def d_hidden(first, last):
        ks = pl.ds(first * TILE, (last - first) * TILE)
        dh[...] += nt(nat[:, ks], wd[:, ks])

    def d_activate():
        dgu[:, : 2 * units] = (dh[...] * a_gate[...]).astype(BF16)
        dgu[:, 2 * units :] = (dh[...] * a_up[...]).astype(BF16)

    def d_inputs(first, last):
        blocked(lambda cols: nt(dgu[...], gu[cols, :]), part_g, first, last)

    def by_quarter(weights):
        quarter_of = (iota(weights.shape, 1) // CAP) & (QUARTERS - 1)
        return jnp.concatenate(
            [jnp.where(quarter_of == q, weights, 0.0).astype(BF16) for q in range(QUARTERS)], axis=0
        )

    def place(left, got, out):
        terms = left.shape[1] // STACK
        for i in range(quarter // COLS):
            block = got[:, :, cols_of(i)].reshape(STACK, COLS)
            total = dot(left, jnp.concatenate([block] * terms, axis=0)).astype(BF16)
            for q in range(QUARTERS):
                out[:, cols_of(i, q)] = total[q * tokens : (q + 1) * tokens]

    def three_terms(weights):
        high = weights.astype(BF16).astype(F32)
        mid = (weights - high).astype(BF16).astype(F32)
        low = (weights - high - mid).astype(BF16).astype(F32)
        ends = jnp.concatenate([low, jnp.zeros_like(low)], axis=0).T
        return jnp.concatenate([jnp.concatenate([high, mid], axis=0).T, ends[:, :STACK]], axis=1)

    tiles = width // TILE
    steps = quarter // COLS

    own[0].wait()
    own[1].start()
    choose(tok, pick_x, None, 0, steps)
    pl.semaphore_wait(barrier, len(peers))
    x_copies = [x_copy(0, pick_x, rows, k) for k in (1, 3, 2)]
    for copy in x_copies:
        copy.start()
    rows[0, 0] = pick_x[x]
    def row_steps(*which):
        for i in which:
            gather_step(0, pick_x, rows, ROWS, i)

    def grad_steps(*which):
        for i in which:
            gather_step(1, pick_g, grads, GRADS, i)

    def out_steps(*which):
        for i in which:
            sum_step(2, part_y, recv_y, i)

    def end_steps(*which):
        for i in which:
            sum_step(3, part_g, recv_g, i)

    row_steps(0)
    own[1].wait()
    for copy in own[2:]:
        copy.start()
    choose(cot, pick_g, jnp.sum(wsel[...], axis=1, keepdims=True), 0, steps)
    g_copies = [x_copy(1, pick_g, grads, k) for k in (1, 3, 2)]
    for copy in g_copies:
        copy.start()
    grads[0, 0] = pick_g[x]
    grad_steps(0)
    row_steps(1, 2)
    grad_steps(1, 2)
    row_steps(3, 4)
    small = [
        remote(wsel, wsel_in, s_send.at[0], s_recv.at[0], up[0]),
        remote(sel, sel_in, s_send.at[1], s_recv.at[1], down[0]),
    ]
    other = [
        remote(wg_ref, gu.at[:, pl.ds(units, units)], w_send.at[0], w_recv.at[0], sibling),
        remote(wu_ref, gu.at[:, pl.ds(3 * units, units)], w_send.at[1], w_recv.at[1], sibling),
        remote(wd_ref, wd.at[pl.ds(units, units)], w_send.at[2], w_recv.at[2], sibling),
    ]
    for copy in other + small:
        copy.start()
    row_steps(5, 6)
    swap[...] = regrouping(0)
    row_steps(7, 8)
    acc[...] = jnp.zeros_like(acc)
    dh[...] = jnp.zeros_like(dh)
    row_steps(9, 10, 11, 12, 13)
    grad_steps(3, 4)
    arrive(0, pick_x, rows, ROWS, RIGHT, 2, 0, FLIGHT)
    natural(rows, 0)
    grad_steps(5)

    gather_end(0, pick_x, rows, ROWS)
    natural(rows, 1)
    for copy in own[2:]:
        copy.wait()
    for copy in other:
        copy.wait_recv()
    grad_steps(6)
    gate_up(0, tiles // 2)
    grad_steps(7, 8)
    gate_up(tiles // 2, tiles)
    activate()
    grad_steps(9, 10)
    outputs(0, 2)
    grad_steps(11)
    outputs(2, 4)
    grad_steps(12)
    outputs(4, 6)
    grad_steps(13)
    outputs(6, steps)

    out_steps(0, 1)
    arrive(1, pick_g, grads, GRADS, RIGHT, 2, 0, FLIGHT)
    natural(grads, 0)
    out_steps(2)
    gather_end(1, pick_g, grads, GRADS)
    natural(grads, 1)
    out_steps(3)
    d_hidden(0, tiles)
    d_activate()
    out_steps(4, 5)
    d_inputs(0, 2)
    out_steps(6, 7)
    d_inputs(2, 4)
    out_steps(8)
    d_inputs(4, 6)
    out_steps(9)
    d_inputs(6, steps)
    end_steps(0, 1)
    out_steps(10)
    end_steps(2, 3)
    small[0].wait_recv()
    weights_y = by_quarter(three_terms(wsel_in[...]))
    small[1].wait_recv()
    left_ref[...] = by_quarter(jnp.concatenate([sel_in[...], jnp.zeros_like(sel_in)], axis=0).T[:, :STACK])
    out_steps(11)
    end_steps(4, 5)
    for copy in x_copies + g_copies + other + small:
        copy.wait_send()
    out_steps(12)
    end_steps(6, 7)
    out_steps(13)
    end_steps(8, 9, 10, 11)
    for i in range(STEPS):
        for way in WAYS:
            gather_copy(0, rows, ROWS, way, i).wait_send()
            gather_copy(1, grads, GRADS, way, i).wait_send()

    done_y = finish(2, part_y, recv_y, got_y, up, LAST)
    end_steps(12, 13)
    for i in range(STEPS):
        for way in WAYS:
            sum_copy(2, part_y, recv_y, way, i).wait_send()
    done_g = finish(3, part_g, recv_g, got_g, down, LAST)
    for i in range(STEPS):
        for way in WAYS:
            sum_copy(3, part_g, recv_g, way, i).wait_send()
    for copy in done_y:
        copy.wait()
    place(weights_y, got_y, out_ref)
    for copy in done_g:
        copy.wait()


def write_out(y_ref, g_ref, left_ref, out_hbm, grad_hbm, dense, sems):
    tokens, width = y_ref.shape
    quarter = width // QUARTERS
    copies = [pltpu.make_async_copy(y_ref, out_hbm, sems.at[3 * QUARTERS])]
    copies[0].start()
    left = left_ref[...]
    cuts = (0, 3, 5, 7)
    for n in range(len(cuts) - 1):
        for i in range(cuts[n], cuts[n + 1]):
            block = g_ref[:, :, i * COLS : (i + 1) * COLS].reshape(STACK, COLS)
            total = dot(left, block).astype(BF16)
            for q in range(QUARTERS):
                dense[:, q * quarter + i * COLS : q * quarter + (i + 1) * COLS] = total[q * tokens : (q + 1) * tokens]
        for q in range(QUARTERS):
            cols = pl.ds(q * quarter + cuts[n] * COLS, (cuts[n + 1] - cuts[n]) * COLS)
            copy = pltpu.make_async_copy(
                dense.at[:, cols], grad_hbm.at[:, cols], sems.at[n * QUARTERS + q]
            )
            copy.start()
            copies.append(copy)
    for copy in copies:
        copy.wait()


def on_device(section_input, cotangent, routes, gate_codes, w_gate, w_up, w_down):
    tokens, width = section_input.shape[1:]
    quarter = width // QUARTERS
    units = w_gate.shape[2]
    count = RING * FLIGHT * CAP
    vmem = pl.BlockSpec(memory_space=pltpu.VMEM)
    hbm = pl.BlockSpec(memory_space=pltpu.HBM)
    dma = pltpu.SemaphoreType.DMA
    blocks = pltpu.VMEM((FLIGHT, UNIT, quarter), BF16)
    gathered = pltpu.VMEM((RING, FLIGHT, UNIT, quarter), BF16)
    incoming = pltpu.VMEM((2, 4, FLIGHT, UNIT, quarter), BF16)
    block = pltpu.VMEM((tokens, width), BF16)
    half_wide = pltpu.VMEM((count, 2 * units), F32)
    select = pltpu.VMEM((STACK, tokens), F32)
    dense = jax.ShapeDtypeStruct((tokens, width), BF16)
    out_dense, got_g, left = pl.pallas_call(
        exchange,
        out_shape=(
            dense,
            jax.ShapeDtypeStruct((FLIGHT, UNIT, quarter), BF16),
            jax.ShapeDtypeStruct((QUARTERS * tokens, STACK), BF16),
        ),
        in_specs=[vmem] + [hbm] * 5,
        out_specs=(vmem,) * 3,
        scratch_shapes=[
            block, block, blocks, blocks, gathered, gathered,
            pltpu.VMEM((count, width), BF16),
            pltpu.VMEM((width, 4 * units), BF16),
            pltpu.VMEM((2 * units, width), BF16),
            pltpu.VMEM((STACK * QUARTERS, STACK * QUARTERS), BF16),
            pltpu.VMEM((count, 4 * units), F32),
            half_wide,
            half_wide,
            pltpu.VMEM((count, 2 * units), BF16),
            half_wide,
            pltpu.VMEM((count, 4 * units), BF16),
            gathered, gathered, incoming, incoming, blocks,
            select, select, select, select,
            dma((5,)),
            dma((3,)), dma((3,)),
            dma((2, FLIGHT)), dma((2, FLIGHT)),
            dma((2,)), dma((2,)),
            dma((4, 2, MOST)), dma((4, 2, MOST)),
            dma((2, FLIGHT)), dma((2, FLIGHT)),
        ],
        compiler_params=pltpu.CompilerParams(
            collective_id=0, has_side_effects=True, vmem_limit_bytes=51 * 2**20
        ),
        cost_estimate=pl.CostEstimate(
            flops=24 * count * width * units, bytes_accessed=14 * tokens * width, transcendentals=0
        ),
        name="exchange",
    )(jnp.concatenate([routes[0].T, gate_codes[0].T]), section_input[0], cotangent[0], w_gate[0], w_up[0], w_down[0])
    passed, grad_passed = pl.pallas_call(
        write_out,
        out_shape=(dense,) * 2,
        in_specs=[vmem] * 3,
        out_specs=(hbm,) * 2,
        scratch_shapes=[block, dma((1 + 3 * QUARTERS,))],
        compiler_params=pltpu.CompilerParams(vmem_limit_bytes=51 * 2**20),
        name="write_out",
    )(out_dense, got_g, left)
    return passed[None], grad_passed[None]


def solution(mesh):
    placed = (
        P("pipe", "expert", None),
        P("pipe", "expert", None),
        P("pipe", "expert", None),
        P("pipe", "expert", None),
        P("pipe", None, "expert"),
        P("pipe", None, "expert"),
        P("pipe", "expert", None),
    )
    return jax.shard_map(
        on_device,
        mesh=mesh,
        in_specs=placed,
        out_specs=(P("pipe", "expert", None), P("pipe", "expert", None)),
        check_vma=False,
    )
```
